128 devices in a mesh: ctx: 8 (over z_hi, y), fsdp: 16 (over x, z_lo, core).
Axes of the slice: x: 4, y: 4, z: 4 (z_hi: 2, z_lo: 2; z = z_hi * 2 + z_lo), core: 2. Of those that a mesh axis runs over, the one named last changes fastest.
Arguments:
- tokens: bfloat16 [16, 2, 512, 2048], P('fsdp', None, 'ctx'), may hold values from -6 to 6
- positions: int32 [16, 2, 512], P('fsdp'), may hold values from 0 to 1023, as said below
- attention_gain: float32 [2048], P('fsdp'), may hold values from 0.5 to 1.5
- query_weight: bfloat16 [2048, 2048], P('fsdp'), may hold values from -0.125 to 0.125
- key_weight: bfloat16 [2048, 256], P('fsdp'), may hold values from -0.125 to 0.125
- value_weight: bfloat16 [2048, 256], P('fsdp'), may hold values from -0.125 to 0.125
- out_weight: bfloat16 [2048, 2048], P('fsdp'), may hold values from -0.5 to 0.5
- feed_gain: float32 [2048], P('fsdp'), may hold values from 0.5 to 1.5
- gate_weight: bfloat16 [2048, 5632], P('fsdp'), may hold values from -0.125 to 0.125
- up_weight: bfloat16 [2048, 5632], P('fsdp'), may hold values from -0.125 to 0.125
- down_weight: bfloat16 [5632, 2048], P('fsdp'), may hold values from -0.078125 to 0.078125
- cotangent: bfloat16 [16, 2, 512, 2048], P('fsdp', None, 'ctx'), may hold values from -6 to 6
Outputs:
- output: bfloat16 [16, 2, 512, 2048], P('fsdp', None, 'ctx')
- tokens_grad: float32 [16, 2, 512, 2048], P('fsdp', None, 'ctx')
- attention_gain_grad: float32 [2048], P('fsdp')
- query_weight_grad: float32 [2048, 2048], P('fsdp')
- key_weight_grad: float32 [2048, 256], P('fsdp')
- value_weight_grad: float32 [2048, 256], P('fsdp')
- out_weight_grad: float32 [2048, 2048], P('fsdp')
- feed_gain_grad: float32 [2048], P('fsdp')
- gate_weight_grad: float32 [2048, 5632], P('fsdp')
- up_weight_grad: float32 [2048, 5632], P('fsdp')
- down_weight_grad: float32 [5632, 2048], P('fsdp')
The draws below stay inside these ranges and needn't reach their ends.
Inputs may be any that keep to these rules, and one draw needn't show every extreme that they name: `positions`: for each sequence a permutation p of the 8 block numbers is drawn: slots (0, c * 64 + i) hold position p(c) * 64 + i and slots (1, c * 64 + i) hold position (15 - p(c)) * 64 + i, for i < 64; every position of a sequence occurs once.
All inputs are finite; a program needn't handle non-finite values.
Results may differ from the reference program's by a relative error of at most 0.038.
Values may be sent and summed in bfloat16 or wider, within the bound.
A program may use at most 320 MiB of HBM per device.

```python
import jax
import jax.numpy as jnp
from jax import lax

D = 2048
FF = 5632
HEADS = 32
KV_HEADS = 4
HEAD_DIM = 64
BLK = 64
HALF = 512
LENGTH = 1024
SEQS = 16
N_CTX = 8


def draw_positions(key, part):
    key = jax.random.fold_in(key, 5)
    seq_keys = jax.random.split(key, SEQS)

    def single(seq_key):
        order = jax.random.permutation(seq_key, N_CTX).astype(jnp.int32)
        blocks = jnp.stack([order, 2 * N_CTX - 1 - order])
        within = jnp.arange(BLK, dtype=jnp.int32)
        return (blocks[:, :, None] * BLK + within[None, None, :]).reshape(2, N_CTX * BLK)
    return jax.vmap(single)(seq_keys)


def block_levels(stream_key, dims, cuts, smallest, top_value):
    loudness = 1.0
    for axis_at, shards_of in cuts:
        heights = jax.random.uniform(jax.random.fold_in(jax.random.fold_in(stream_key, 6), axis_at), (shards_of,), jnp.float32, smallest / len(cuts), top_value / len(cuts))
        loudness = loudness * jnp.repeat(jnp.exp(heights), dims[axis_at] // shards_of).reshape((-1,) + (1,) * (len(dims) - 1 - axis_at))
    return loudness


def gaussian(key, extent, scale, bound, cuts=(), held_as=jnp.bfloat16):
    gain = block_levels(key, extent, cuts, -0.22, 0.18) if cuts else 1.0
    values = jax.random.normal(key, extent, jnp.float32) * scale * gain
    return jnp.minimum(jnp.maximum(values, -bound), bound).astype(held_as)


def setup_inputs(seed: int = 0) -> dict:
    seeds = jax.random.split(jax.random.key(seed), 13)
    return {
        "tokens": gaussian(seeds[0], (SEQS, 2, HALF, D), 1.0, 6.0, ((0, 16), (2, 8))),
        "positions": draw_positions(jax.random.fold_in(seeds[12], 71), 0),
        "attention_gain": jnp.clip(1.0 + 0.1 * jax.random.normal(seeds[2], (D,), jnp.float32), 0.5, 1.5),
        "query_weight": gaussian(seeds[3], (D, HEADS * HEAD_DIM), D ** -0.5, 0.125, ((0, 16),)),
        "key_weight": gaussian(seeds[4], (D, KV_HEADS * HEAD_DIM), D ** -0.5, 0.125, ((0, 16),)),
        "value_weight": gaussian(seeds[5], (D, KV_HEADS * HEAD_DIM), D ** -0.5, 0.125, ((0, 16),)),
        "out_weight": gaussian(seeds[6], (HEADS * HEAD_DIM, D), (HEADS * HEAD_DIM // 16) ** -0.5, 0.5, ((0, 16),)),
        "feed_gain": jnp.clip(1.0 + 0.1 * jax.random.normal(seeds[7], (D,), jnp.float32), 0.5, 1.5),
        "gate_weight": gaussian(seeds[8], (D, FF), D ** -0.5, 0.125, ((0, 16),)),
        "up_weight": gaussian(seeds[9], (D, FF), D ** -0.5, 0.125, ((0, 16),)),
        "down_weight": gaussian(seeds[10], (FF, D), FF ** -0.5, 0.078125, ((0, 16),)),
        "cotangent": gaussian(seeds[11], (SEQS, 2, HALF, D), 1.0, 6.0, ((0, 16), (2, 8))),
    }


@jax.custom_vjp
def low(v):
    return lax.optimization_barrier(v.astype(jnp.bfloat16)).astype(jnp.float32)

@jax.custom_vjp
def low_back(v):
    return v

def low_keep(v):
    return (low(v), None)

def low_pass(kept, grad):
    return (grad,)

def back_keep(v):
    return (v, None)

def back_low(kept, grad):
    return (low(grad),)
low.defvjp(low_keep, low_pass)
low_back.defvjp(back_keep, back_low)
highest = lax.Precision.HIGHEST
epsilon = 1e-05

def matmul(left, right):
    return jnp.matmul(left, right, precision=highest)

def frequencies(head_width):
    return 10000.0 ** (-(2.0 * jnp.arange(head_width // 2, dtype=jnp.float32)) / head_width)

def normalize(values, gain_vector):
    scaled = lax.rsqrt(lax.optimization_barrier(jnp.mean(values * values, axis=-1, keepdims=True)) + epsilon)
    return values * scaled * gain_vector

def rotate(field, cosine, sine_part):
    middle = field.shape[-1] // 2
    former = field[..., :middle]
    latter = field[..., middle:]
    cosine = cosine[..., None, :]
    sine_part = sine_part[..., None, :]
    return jnp.concatenate([former * cosine - latter * sine_part, latter * cosine + former * sine_part], axis=-1)

def attend(queries, keys_all, values_all):
    length = queries.shape[0]
    grouped = queries.reshape(length, KV_HEADS, HEADS // KV_HEADS, HEAD_DIM)
    scores = low_back(jnp.einsum('qkgd,lkd->kgql', grouped, keys_all, precision=highest) * 0.125)
    places = jnp.arange(length)
    allowed = places[None, :] <= places[:, None]
    scores = jnp.where(allowed, scores, -1e+30)
    largest = lax.optimization_barrier(jnp.max(scores, axis=-1, keepdims=True))
    weights = jnp.exp(scores - largest)
    weights = weights / lax.optimization_barrier(jnp.sum(weights, axis=-1, keepdims=True))
    mixed = jnp.einsum('kgql,lkd->qkgd', low(weights), values_all, precision=highest)
    return mixed.reshape(length, HEADS * HEAD_DIM)

def layer(hidden_in, attention_gain, query_weight, key_weight, value_weight, out_weight, feed_gain, gate_weight, up_weight, down_weight):
    length = hidden_in.shape[0]
    angles = jnp.arange(length, dtype=jnp.float32)[:, None] * frequencies(HEAD_DIM)[None, :]
    cosine = jnp.cos(angles)
    sine_part = jnp.sin(angles)
    normed = low(normalize(hidden_in, attention_gain))
    queries = low_back(matmul(normed, query_weight)).reshape(length, HEADS, HEAD_DIM)
    queries = low(rotate(queries, cosine, sine_part))
    keys_all = low_back(matmul(normed, key_weight)).reshape(length, KV_HEADS, HEAD_DIM)
    keys_all = low(rotate(keys_all, cosine, sine_part))
    values_all = low(low_back(matmul(normed, value_weight))).reshape(length, KV_HEADS, HEAD_DIM)
    mixed = attend(queries, keys_all, values_all)
    branch = low_back(matmul(low(low_back(mixed)), out_weight))
    residual = hidden_in + branch
    normed_two = low(normalize(residual, feed_gain))
    gate = low_back(matmul(normed_two, gate_weight))
    upward = low_back(matmul(normed_two, up_weight))
    product = low(jax.nn.silu(gate) * upward)
    return residual + low_back(matmul(product, down_weight))

def reference(tokens, positions, attention_gain, query_weight, key_weight, value_weight, out_weight, feed_gain, gate_weight, up_weight, down_weight, cotangent):
    seq_count = tokens.shape[0]
    width = tokens.shape[-1]
    places = positions.reshape(seq_count, LENGTH).astype(jnp.int32)
    counting = jnp.broadcast_to(jnp.arange(LENGTH, dtype=jnp.int32)[None, :], (seq_count, LENGTH))
    slots = jnp.zeros((seq_count, LENGTH), jnp.int32).at[jnp.arange(seq_count)[:, None], places].set(counting)
    flat = tokens.astype(jnp.float32).reshape(seq_count, LENGTH, width)
    ordered = jnp.take_along_axis(flat, slots[:, :, None], axis=1)
    seed_grad = jnp.take_along_axis(cotangent.astype(jnp.float32).reshape(seq_count, LENGTH, width), slots[:, :, None], axis=1)

    def forward(hidden_in, gain_one, query_w, key_w, value_w, out_w, gain_two, gate_w, up_w, down_w):

        def single(sequence):
            return layer(sequence, gain_one, query_w, key_w, value_w, out_w, gain_two, gate_w, up_w, down_w)
        return lax.map(jax.checkpoint(single), hidden_in)
    result, pullback = jax.vjp(forward, ordered, attention_gain.astype(jnp.float32), query_weight.astype(jnp.float32), key_weight.astype(jnp.float32), value_weight.astype(jnp.float32), out_weight.astype(jnp.float32), feed_gain.astype(jnp.float32), gate_weight.astype(jnp.float32), up_weight.astype(jnp.float32), down_weight.astype(jnp.float32))
    grads = pullback(seed_grad)
    output = jnp.take_along_axis(result, places[:, :, None], axis=1).reshape(tokens.shape).astype(jnp.bfloat16)
    tokens_grad = jnp.take_along_axis(grads[0], places[:, :, None], axis=1).reshape(tokens.shape)
    return (output, tokens_grad, grads[1], grads[2], grads[3], grads[4], grads[5], grads[6], grads[7], grads[8], grads[9])
```

```python
import jax
import jax.numpy as jnp
from jax import lax
from jax.sharding import PartitionSpec as P

HEAD_DIM = 64
BF = jnp.bfloat16
F32 = jnp.float32
epsilon = 1e-05
AXES = ("ctx", "fsdp")


def table(step):
    pairs = []
    for c in range(8):
        for f in range(16):
            c2, f2 = step(c, f)
            pairs.append((c * 16 + f, c2 * 16 + f2))
    return pairs


CORE = table(lambda c, f: (c, f ^ 1))
Z_IN = table(lambda c, f: (c, f ^ 2))
Z_OUT = table(lambda c, f: (c ^ 4, f ^ 2))
Z_HI = table(lambda c, f: (c ^ 4, f))
X_UP = table(lambda c, f: (c, (f + 4) & 15))
X_DOWN = table(lambda c, f: (c, (f + 12) & 15))
X_FAR = table(lambda c, f: (c, f ^ 8))
X_NEAR = table(lambda c, f: (c, f ^ 4))
Y_UP = table(lambda c, f: ((c & 4) | ((c + 1) & 3), f))
Y_DOWN = table(lambda c, f: ((c & 4) | ((c + 3) & 3), f))
Y_FAR = table(lambda c, f: (c ^ 2, f))
Y_NEAR = table(lambda c, f: (c ^ 1, f))


def move(a, pairs):
    return lax.ppermute(a, AXES, pairs)


def dot(a, b):
    return jnp.dot(a, b, preferred_element_type=F32)


def dot_t(a, b):
    return lax.dot_general(a, b, (((1,), (1,)), ((), ())), preferred_element_type=F32)


def t_dot(a, b):
    return lax.dot_general(a, b, (((0,), (0,)), ((), ())), preferred_element_type=F32)


def pick(a, index, axis=0):
    return lax.dynamic_index_in_dim(a, index, axis, keepdims=False)


def put(blocks, places, like):
    out = jnp.zeros((len(blocks),) + blocks[0].shape, like)
    for block, place in zip(blocks, places):
        out = lax.dynamic_update_index_in_dim(out, block.astype(like), place, 0)
    return out


class Where:
    def __init__(self):
        ctx, fsdp = lax.axis_index("ctx"), lax.axis_index("fsdp")
        self.ctx = ctx
        self.y = lax.rem(ctx, 4)
        self.hi = ctx // 4
        self.fsdp = fsdp
        self.x = fsdp // 4
        self.z = lax.rem(fsdp // 2, 2)
        self.c = lax.rem(fsdp, 2)


def cyc(i, d):
    return lax.rem(i + d + 4, 4)


def to_rel(a, at):
    blocks = [a[:, 128 * i : 128 * (i + 1)] for i in range(16)]
    order = lambda cf, zf: jnp.concatenate(
        [
            blocks[x * 4 + (z ^ zf) * 2 + (c ^ cf)]
            for c in range(2)
            for z in range(2)
            for x in range(4)
        ],
        axis=1,
    )
    return jnp.where(
        at.c == 0,
        jnp.where(at.z == 0, order(0, 0), order(0, 1)),
        jnp.where(at.z == 0, order(1, 0), order(1, 1)),
    )


def to_abs(a, at):
    blocks = [a[:, 128 * i : 128 * (i + 1)] for i in range(16)]
    order = lambda cf, zf: jnp.concatenate(
        [
            blocks[(c ^ cf) * 8 + (z ^ zf) * 4 + x]
            for x in range(4)
            for z in range(2)
            for c in range(2)
        ],
        axis=1,
    )
    return jnp.where(
        at.c == 0,
        jnp.where(at.z == 0, order(0, 0), order(0, 1)),
        jnp.where(at.z == 0, order(1, 0), order(1, 1)),
    )


def gather_x(a):
    return jnp.concatenate([a, move(a, X_UP), move(a, X_DOWN), move(a, X_FAR)], axis=0)


def scatter_x(parts):
    low = parts.astype(BF)
    got = [move(low[1], X_DOWN), move(low[2], X_UP), move(low[3], X_FAR)]
    return parts[0] + got[0].astype(F32) + got[1].astype(F32) + got[2].astype(F32)


def column_weights(slices, at):
    mine = slices[0]
    from_down, from_up, far = (
        move(slices[1], X_UP),
        move(slices[2], X_DOWN),
        move(slices[3], X_FAR),
    )
    width = mine.shape[1]
    stack = put(
        [mine, from_down, from_up, far],
        [at.x, cyc(at.x, -1), cyc(at.x, 1), cyc(at.x, 2)],
        BF,
    ).reshape(512, width)
    half = jnp.concatenate(
        [stack, move(stack[:256], Z_IN), move(stack[256:], Z_OUT)], axis=0
    )
    return half, move(half, CORE)


def row_weights(own, at):
    rows = own.shape[0]
    half = rows // 2
    other = jnp.concatenate([move(own[:half], Z_IN), move(own[half:], Z_OUT)], axis=0)
    pair = jnp.stack([own, other])
    sibling = move(pair, CORE)
    me = at.z * 2 + at.c
    out = put(
        [own, other, sibling[0], sibling[1]], [me, me ^ 2, me ^ 1, me ^ 3], BF
    )
    return out.reshape(4 * rows, own.shape[1])


def sum_y(pieces, at, axis):
    wide = pick(pieces, at.y, axis).astype(F32)
    got = [
        move(pick(pieces, cyc(at.y, 1), axis), Y_UP),
        move(pick(pieces, cyc(at.y, -1), axis), Y_DOWN),
        move(pick(pieces, cyc(at.y, 2), axis), Y_FAR),
    ]
    total = (wide + got[0].astype(F32) + got[1].astype(F32) + got[2].astype(F32)).astype(BF)
    return total.astype(F32) + move(total, Z_HI).astype(F32)


def gather_y(own, at):
    return put(
        [own, move(own, Y_UP), move(own, Y_DOWN), move(own, Y_FAR)],
        [at.y, cyc(at.y, -1), cyc(at.y, 1), cyc(at.y, 2)],
        BF,
    )


def column_grads(half, other, at):
    width = half.shape[1]
    got = move(other, CORE)
    keep = half[:512].astype(F32) + got[:512].astype(F32)
    send = (half[512:].astype(F32) + got[512:].astype(F32)).astype(BF)
    keep = (
        keep
        + jnp.concatenate([move(send[:256], Z_IN), move(send[256:], Z_OUT)], axis=0).astype(F32)
    ).astype(BF)
    total = sum_y(keep.reshape(4, 4, 32, width), at, 1).astype(BF)
    own = pick(total, at.x)
    ranks = put(
        [
            own,
            move(pick(total, cyc(at.x, 1)), X_UP),
            move(pick(total, cyc(at.x, -1)), X_DOWN),
            move(pick(total, cyc(at.x, 2)), X_FAR),
        ],
        [at.x, cyc(at.x, -1), cyc(at.x, 1), cyc(at.x, 2)],
        BF,
    )
    return gather_y(ranks, at).transpose(0, 2, 1, 3).reshape(128, 4, width)


def row_grads(terms, at):
    width = terms.shape[1]
    rows = terms.shape[0] // 4
    terms = terms.reshape(2, 2, rows, width)
    got = move(pick(terms, 1 - at.c, 1), CORE)
    pair = pick(terms, at.c, 1).astype(F32) + got.astype(F32)
    send = pick(pair, 1 - at.z).astype(BF)
    half = rows // 2
    keep = (
        pick(pair, at.z)
        + jnp.concatenate([move(send[:half], Z_IN), move(send[half:], Z_OUT)], axis=0).astype(F32)
    ).astype(BF)
    total = sum_y(keep.reshape(4, rows // 4, width), at, 0).astype(BF)
    return gather_y(total, at).reshape(rows, width).astype(F32)


def frequencies(head_width):
    return 10000.0 ** (-(2.0 * jnp.arange(head_width // 2, dtype=F32)) / head_width)


def rotate(field, cosine, sine_part):
    middle = field.shape[-1] // 2
    former = field[..., :middle]
    latter = field[..., middle:]
    return jnp.concatenate(
        [former * cosine - latter * sine_part, latter * cosine + former * sine_part], axis=-1
    )


def norm_forward(values, gain_vector):
    scaled = lax.rsqrt(jnp.mean(values * values, axis=-1, keepdims=True) + epsilon)
    return (values * scaled * gain_vector, scaled)


def norm_backward(values, scaled, gain_vector, grad_out):
    weighted = grad_out * gain_vector
    gain_grad = jnp.sum(grad_out * values * scaled, axis=0)
    inner = jnp.mean(weighted * values, axis=-1, keepdims=True)
    return (weighted * scaled - values * scaled * scaled * scaled * inner, gain_grad)


def masked_scores(queries, keys_all, query_places, key_places):
    scores = (
        jnp.einsum("sqgd,skd->sgqk", queries, keys_all, preferred_element_type=F32) * 0.125
    )
    allowed = key_places[:, None, None, :] <= query_places[:, None, :, None]
    return jnp.where(allowed, scores, -1e30)


def attend_forward(queries, keys_all, values_all, query_places, key_places):
    scores = masked_scores(queries, keys_all, query_places, key_places)
    largest = jnp.max(scores, axis=-1, keepdims=True)
    weights = jnp.exp(scores - largest)
    totals = jnp.sum(weights, axis=-1, keepdims=True)
    probs = (weights / totals).astype(BF)
    mixed = jnp.einsum("sgqk,skd->sqgd", probs, values_all, preferred_element_type=F32)
    return (mixed, largest + jnp.log(totals))


def attend_backward(queries, keys_all, values_all, query_places, key_places, log_totals, mixed_grad):
    scores = masked_scores(queries, keys_all, query_places, key_places)
    probs = jnp.exp(scores - log_totals)
    prob_grad = jnp.einsum("sqgd,skd->sgqk", mixed_grad, values_all, preferred_element_type=F32)
    inner = jnp.sum(probs * prob_grad, axis=-1, keepdims=True)
    score_grad = (probs * (prob_grad - inner)).astype(BF)
    query_grad = (
        jnp.einsum("sgqk,skd->sqgd", score_grad, keys_all, preferred_element_type=F32) * 0.125
    )
    key_grad = (
        jnp.einsum("sgqk,sqgd->skd", score_grad, queries, preferred_element_type=F32) * 0.125
    )
    value_grad = jnp.einsum(
        "sgqk,sqgd->skd", probs.astype(BF), mixed_grad, preferred_element_type=F32
    )
    return (query_grad, key_grad, value_grad)


def columns(weight, rank, count):
    return lax.dynamic_slice_in_dim(weight, rank * count, count, 1)


def per_device(
    tokens,
    positions,
    attention_gain,
    query_weight,
    key_weight,
    value_weight,
    out_weight,
    feed_gain,
    gate_weight,
    up_weight,
    down_weight,
    cotangent,
):
    at = Where()
    width = tokens.shape[3]
    heads = query_weight.shape[1] // HEAD_DIM // 4
    hidden = gate_weight.shape[1] // 4
    ranks = [at.x, cyc(at.x, 1), cyc(at.x, -1), cyc(at.x, 2)]

    gains = jnp.stack([attention_gain, feed_gain])
    gains = jnp.stack([gains, move(gains, CORE)])
    gains = jnp.stack([gains, move(gains, Z_IN)])
    gains = put(
        [gains, move(gains, X_UP), move(gains, X_DOWN), move(gains, X_FAR)],
        [at.x, cyc(at.x, -1), cyc(at.x, 1), cyc(at.x, 2)],
        F32,
    )
    gains = jnp.where(at.z == 0, gains, gains[:, ::-1])
    gains = jnp.where(at.c == 0, gains, gains[:, :, ::-1])
    gains = gains.transpose(3, 0, 1, 2, 4).reshape(2, width)
    gain_one, gain_two = gains[0], gains[1]

    places4 = gather_x(positions)
    own_places = lax.dynamic_slice_in_dim(places4, at.ctx * 64, 64, 2).reshape(4, 128)
    key_places = jnp.concatenate(
        [
            lax.dynamic_slice_in_dim(
                places4, (h * 4 + cyc(at.y, d)) * 64, 64, 2
            ).reshape(4, 128)
            for d in (0, -1, 1, 2)
            for h in (at.hi, 1 - at.hi)
        ],
        axis=1,
    )
    angles = own_places.astype(F32)[:, :, None] * frequencies(HEAD_DIM)
    cosine, sine_part = jnp.cos(angles), jnp.sin(angles)

    hidden_in = tokens.reshape(128, width).astype(F32)
    normed_raw, scale_one = norm_forward(hidden_in, gain_one)
    normed = gather_x(to_rel(normed_raw.astype(BF), at))

    first_half, first_other = column_weights(
        [
            jnp.concatenate(
                [
                    columns(query_weight, r, heads * HEAD_DIM),
                    columns(key_weight, r, HEAD_DIM),
                    columns(value_weight, r, HEAD_DIM),
                ],
                axis=1,
            )
            for r in ranks
        ],
        at,
    )
    full_out = row_weights(out_weight, at)
    feed_half, feed_other = column_weights(
        [
            jnp.concatenate(
                [columns(gate_weight, r, hidden), columns(up_weight, r, hidden)], axis=1
            )
            for r in ranks
        ],
        at,
    )
    full_down = row_weights(down_weight, at)
    branch_grad = cotangent.reshape(128, width)
    branch4 = gather_x(branch_grad)

    projected = dot(normed[:, :1024], first_half) + dot(normed[:, 1024:], first_other)
    q_width = heads * HEAD_DIM
    query_rot = rotate(
        projected[:, :q_width].reshape(4, 128, heads, HEAD_DIM),
        cosine[:, :, None],
        sine_part[:, :, None],
    ).astype(BF)
    key_rot = rotate(
        projected[:, q_width : q_width + HEAD_DIM].reshape(4, 128, HEAD_DIM), cosine, sine_part
    ).astype(BF)
    value_low = projected[:, q_width + HEAD_DIM :].reshape(4, 128, HEAD_DIM).astype(BF)
    pair = jnp.concatenate([key_rot, value_low], axis=-1)
    pair = jnp.concatenate([pair, move(pair, Z_HI)], axis=1)
    pair = jnp.concatenate(
        [pair, move(pair, Y_UP), move(pair, Y_DOWN), move(pair, Y_FAR)], axis=1
    )
    key_seq, value_seq = pair[..., :HEAD_DIM], pair[..., HEAD_DIM:]
    mixed, log_totals = attend_forward(query_rot, key_seq, value_seq, own_places, key_places)
    mixed_low = mixed.reshape(512, q_width).astype(BF)
    residual = hidden_in + scatter_x(dot(mixed_low, full_out).reshape(4, 128, width))

    normed_two_raw, scale_two = norm_forward(residual, gain_two)
    normed_two = gather_x(to_rel(normed_two_raw.astype(BF), at))
    two_half, two_other = normed_two[:, :1024], normed_two[:, 1024:]
    both = dot(two_half, feed_half) + dot(two_other, feed_other)
    gate, upward = both[:, :hidden], both[:, hidden:]
    sigmoid_gate = jax.nn.sigmoid(gate)
    activated = gate * sigmoid_gate
    product = (activated * upward).astype(BF)
    product_grad = dot_t(branch4, full_down)
    slope = sigmoid_gate * (1.0 + gate * (1.0 - sigmoid_gate))
    both_grad = jnp.concatenate(
        [
            (product_grad * upward * slope).astype(BF),
            (product_grad * activated).astype(BF),
        ],
        axis=1,
    )
    normed_two_grad = to_abs(
        scatter_x(
            jnp.concatenate(
                [dot_t(both_grad, feed_half), dot_t(both_grad, feed_other)], axis=1
            ).reshape(4, 128, width)
        ),
        at,
    )
    norm_two_back, gain_two_term = norm_backward(residual, scale_two, gain_two, normed_two_grad)
    residual_grad = branch_grad.astype(F32) + norm_two_back

    result = residual + scatter_x(dot(product, full_down).reshape(4, 128, width))
    output = result.astype(BF).reshape(tokens.shape)
    down_sum = row_grads(t_dot(product, branch4).astype(BF), at)
    both_sum = column_grads(
        t_dot(two_half, both_grad).astype(BF), t_dot(two_other, both_grad).astype(BF), at
    ).astype(F32)

    branch_low = gather_x(residual_grad.astype(BF))
    mixed_grad = dot_t(branch_low, full_out).astype(BF)
    out_sum = row_grads(t_dot(mixed_low, branch_low).astype(BF), at)
    query_grad, key_grad, value_grad = attend_backward(
        query_rot,
        key_seq,
        value_seq,
        own_places,
        key_places,
        log_totals,
        mixed_grad.reshape(4, 128, heads, HEAD_DIM),
    )
    pair_grad = jnp.concatenate([key_grad, value_grad], axis=-1).reshape(4, 4, 256, 2 * HEAD_DIM)
    low = pair_grad.astype(BF)
    pair_grad = (
        pair_grad[:, 0]
        + move(low[:, 1], Y_DOWN).astype(F32)
        + move(low[:, 2], Y_UP).astype(F32)
        + move(low[:, 3], Y_FAR).astype(F32)
    )
    pair_grad = pair_grad[:, :128] + move(pair_grad[:, 128:].astype(BF), Z_HI).astype(F32)
    query_pre = rotate(query_grad, cosine[:, :, None], -sine_part[:, :, None]).astype(BF)
    key_pre = rotate(pair_grad[..., :HEAD_DIM], cosine, -sine_part).astype(BF)
    value_pre = pair_grad[..., HEAD_DIM:].astype(BF)
    pre = jnp.concatenate(
        [query_pre.reshape(512, q_width), key_pre.reshape(512, HEAD_DIM), value_pre.reshape(512, HEAD_DIM)],
        axis=1,
    )
    normed_grad = to_abs(
        scatter_x(
            jnp.concatenate([dot_t(pre, first_half), dot_t(pre, first_other)], axis=1).reshape(
                4, 128, width
            )
        ),
        at,
    )
    norm_one_back, gain_one_term = norm_backward(hidden_in, scale_one, gain_one, normed_grad)
    input_grad = residual_grad + norm_one_back
    first_sum = column_grads(
        t_dot(normed[:, :1024], pre).astype(BF), t_dot(normed[:, 1024:], pre).astype(BF), at
    ).astype(F32)

    terms = jnp.stack([gain_one_term, gain_two_term])
    for pairs in (CORE, Z_IN, Z_HI, X_NEAR, X_FAR, Y_NEAR, Y_FAR):
        terms = terms + move(terms, pairs)
    terms = lax.dynamic_slice_in_dim(terms, at.fsdp * 128, 128, 1)
    return (
        output,
        input_grad.reshape(tokens.shape),
        terms[0],
        first_sum[:, :, :q_width].reshape(128, -1),
        first_sum[:, :, q_width : q_width + HEAD_DIM].reshape(128, -1),
        first_sum[:, :, q_width + HEAD_DIM :].reshape(128, -1),
        out_sum,
        terms[1],
        both_sum[:, :, :hidden].reshape(128, -1),
        both_sum[:, :, hidden:].reshape(128, -1),
        down_sum,
    )


def solution(mesh):
    rows = P("fsdp", None)
    blocks = P("fsdp", None, "ctx", None)
    return jax.shard_map(
        per_device,
        mesh=mesh,
        in_specs=(
            blocks,
            P("fsdp", None, None),
            P("fsdp"),
            rows,
            rows,
            rows,
            rows,
            P("fsdp"),
            rows,
            rows,
            rows,
            blocks,
        ),
        out_specs=(blocks, blocks, P("fsdp"), rows, rows, rows, rows, P("fsdp"), rows, rows, rows),
        check_vma=False,
    )
```

```python
import jax
import jax.numpy as jnp
from jax import lax
from jax.experimental import pallas as pl
from jax.experimental.pallas import tpu as pltpu
from jax.sharding import PartitionSpec as P

HEAD_DIM = 64
BF = jnp.bfloat16
F32 = jnp.float32
epsilon = 1e-05
AXES = ("ctx", "fsdp")


def table(step):
    pairs = []
    for c in range(8):
        for f in range(16):
            c2, f2 = step(c, f)
            pairs.append((c * 16 + f, c2 * 16 + f2))
    return pairs


CORE = table(lambda c, f: (c, f ^ 1))
Z_IN = table(lambda c, f: (c, f ^ 2))
Z_OUT = table(lambda c, f: (c ^ 4, f ^ 2))
Z_HI = table(lambda c, f: (c ^ 4, f))
X_UP = table(lambda c, f: (c, (f + 4) & 15))
X_DOWN = table(lambda c, f: (c, (f + 12) & 15))
X_FAR = table(lambda c, f: (c, f ^ 8))
X_NEAR = table(lambda c, f: (c, f ^ 4))
Y_UP = table(lambda c, f: ((c & 4) | ((c + 1) & 3), f))
Y_DOWN = table(lambda c, f: ((c & 4) | ((c + 3) & 3), f))
Y_FAR = table(lambda c, f: (c ^ 2, f))
Y_NEAR = table(lambda c, f: (c ^ 1, f))


def move(a, pairs):
    return lax.ppermute(a, AXES, pairs)


def dot(a, b):
    return jnp.dot(a, b, preferred_element_type=F32)


def dot_t(a, b):
    return lax.dot_general(a, b, (((1,), (1,)), ((), ())), preferred_element_type=F32)


def t_dot(a, b):
    return lax.dot_general(a, b, (((0,), (0,)), ((), ())), preferred_element_type=F32)


def pick(a, index, axis=0):
    return lax.dynamic_index_in_dim(a, index, axis, keepdims=False)


def put(blocks, places, like):
    out = jnp.zeros((len(blocks),) + blocks[0].shape, like)
    for block, place in zip(blocks, places):
        out = lax.dynamic_update_index_in_dim(out, block.astype(like), place, 0)
    return out


class Where:
    def __init__(self):
        ctx, fsdp = lax.axis_index("ctx"), lax.axis_index("fsdp")
        self.ctx = ctx
        self.y = lax.rem(ctx, 4)
        self.hi = ctx // 4
        self.fsdp = fsdp
        self.x = fsdp // 4
        self.z = lax.rem(fsdp // 2, 2)
        self.c = lax.rem(fsdp, 2)


def cyc(i, d):
    return lax.rem(i + d + 4, 4)


def gather_x(a):
    return jnp.concatenate([a, move(a, X_UP), move(a, X_DOWN), move(a, X_FAR)], axis=0)


def scatter_x(parts):
    low = parts.astype(BF)
    got = [move(low[1], X_DOWN), move(low[2], X_UP), move(low[3], X_FAR)]
    return parts[0] + got[0].astype(F32) + got[1].astype(F32) + got[2].astype(F32)


def sum_y(pieces, at, axis):
    wide = pick(pieces, at.y, axis).astype(F32)
    got = [
        move(pick(pieces, cyc(at.y, 1), axis), Y_UP),
        move(pick(pieces, cyc(at.y, -1), axis), Y_DOWN),
        move(pick(pieces, cyc(at.y, 2), axis), Y_FAR),
    ]
    total = (wide + got[0].astype(F32) + got[1].astype(F32) + got[2].astype(F32)).astype(BF)
    return total.astype(F32) + move(total, Z_HI).astype(F32)


def gather_y(own, at):
    return put(
        [own, move(own, Y_UP), move(own, Y_DOWN), move(own, Y_FAR)],
        [at.y, cyc(at.y, -1), cyc(at.y, 1), cyc(at.y, 2)],
        BF,
    )


def column_grads(terms, at):
    width = terms.shape[1]
    terms = terms.reshape(4, 2, 2, 128, width)
    got = move(pick(terms, 1 - at.c, 2), CORE)
    pair = pick(terms, at.c, 2).astype(F32) + got.astype(F32)
    send = pick(pair, 1 - at.z, 1).astype(BF)
    keep = (
        pick(pair, at.z, 1)
        + jnp.concatenate([move(send[:2], Z_IN), move(send[2:], Z_OUT)], axis=0).astype(F32)
    ).astype(BF)
    total = sum_y(keep.reshape(4, 4, 32, width), at, 1).astype(BF)
    own = pick(total, at.x)
    ranks = put(
        [
            own,
            move(pick(total, cyc(at.x, 1)), X_UP),
            move(pick(total, cyc(at.x, -1)), X_DOWN),
            move(pick(total, cyc(at.x, 2)), X_FAR),
        ],
        [at.x, cyc(at.x, -1), cyc(at.x, 1), cyc(at.x, 2)],
        BF,
    )
    return gather_y(ranks, at).transpose(0, 2, 1, 3).reshape(128, 4, width)


def row_grads(terms, at):
    width = terms.shape[1]
    rows = terms.shape[0] // 4
    terms = terms.reshape(2, 2, rows, width)
    got = move(pick(terms, 1 - at.c, 1), CORE)
    pair = pick(terms, at.c, 1).astype(F32) + got.astype(F32)
    send = pick(pair, 1 - at.z).astype(BF)
    half = rows // 2
    keep = (
        pick(pair, at.z)
        + jnp.concatenate([move(send[:half], Z_IN), move(send[half:], Z_OUT)], axis=0).astype(F32)
    ).astype(BF)
    total = sum_y(keep.reshape(4, rows // 4, width), at, 0).astype(BF)
    return gather_y(total, at).reshape(rows, width).astype(F32)


def frequencies(head_width):
    return 10000.0 ** (-(2.0 * jnp.arange(head_width // 2, dtype=F32)) / head_width)


def rotate(field, cosine, sine_part):
    middle = field.shape[-1] // 2
    former = field[..., :middle]
    latter = field[..., middle:]
    return jnp.concatenate(
        [former * cosine - latter * sine_part, latter * cosine + former * sine_part], axis=-1
    )


def norm_backward(values, scaled, gain_vector, grad_out):
    weighted = grad_out * gain_vector
    gain_grad = jnp.sum(grad_out * values * scaled, axis=0)
    inner = jnp.mean(weighted * values, axis=-1, keepdims=True)
    return (weighted * scaled - values * scaled * scaled * scaled * inner, gain_grad)


def attend_backward(queries, keys_all, values_all, query_places, key_places, log_totals, mixed_grad):
    scores = jnp.einsum("sqgd,skd->sgqk", queries, keys_all, preferred_element_type=F32)
    allowed = key_places[:, None, None, :] <= query_places[:, None, :, None]
    probs = jnp.exp(jnp.where(allowed, scores, -1e30) - log_totals)
    prob_grad = jnp.einsum("sqgd,skd->sgqk", mixed_grad, values_all, preferred_element_type=F32)
    inner = jnp.sum(probs * prob_grad, axis=-1, keepdims=True)
    score_grad = (probs * (prob_grad - inner)).astype(BF)
    query_grad = (
        jnp.einsum("sgqk,skd->sqgd", score_grad, keys_all, preferred_element_type=F32) * 0.125
    )
    key_grad = jnp.einsum("sgqk,sqgd->skd", score_grad, queries, preferred_element_type=F32)
    value_grad = jnp.einsum(
        "sgqk,sqgd->skd", probs.astype(BF), mixed_grad, preferred_element_type=F32
    )
    return (query_grad, key_grad, value_grad)


MESH = pl.DeviceIdType.MESH
EVERYWHERE = pl.BlockSpec(memory_space=pl.ANY)
ON_CHIP = pl.BlockSpec(memory_space=pltpu.VMEM)
VMEM_LIMIT = 62 * 2**20


class Spot:
    def __init__(self):
        ctx, f = lax.axis_index("ctx"), lax.axis_index("fsdp")
        self.ctx, self.f = ctx, f
        self.y, self.hi = lax.rem(ctx, 4), ctx // 4
        self.x, self.z, self.c = f // 4, lax.rem(f // 2, 2), lax.rem(f, 2)
        self.zc = lax.rem(f, 4)

    def xs(self, d):
        return lax.rem(self.x + d, 4)

    def ys(self, d):
        return lax.rem(self.y + d, 4)

    def to_x(self, d):
        return (self.ctx, self.xs(d) * 4 + self.zc)

    def to_y(self, d):
        return (self.hi * 4 + self.ys(d), self.f)

    def z_in(self):
        return (self.ctx, self.x * 4 + (1 - self.z) * 2 + self.c)

    def z_out(self):
        return ((1 - self.hi) * 4 + self.y, self.x * 4 + (1 - self.z) * 2 + self.c)

    def z_hi(self):
        return ((1 - self.hi) * 4 + self.y, self.f)

    def core(self):
        return (self.ctx, self.x * 4 + self.z * 2 + 1 - self.c)

    def fsdp(self, d):
        return (self.ctx, lax.rem(self.f + d, 16))


class Copies:
    def __init__(self, send_sems, recv_sems, local_sems):
        self.send_sems, self.recv_sems, self.local_sems = send_sems, recv_sems, local_sems
        self.count = self.local_count = 0
        self.started = []

    def send(self, source, target, peer):
        copy = pltpu.make_async_remote_copy(
            src_ref=source,
            dst_ref=target,
            send_sem=self.send_sems.at[self.count],
            recv_sem=self.recv_sems.at[self.count],
            device_id=peer,
            device_id_type=MESH,
        )
        self.count += 1
        copy.start()
        self.started.append(copy)
        return copy

    def local(self, source, target):
        copy = pltpu.make_async_copy(source, target, self.local_sems.at[self.local_count])
        self.local_count += 1
        copy.start()
        return copy

    def finish(self):
        for copy in self.started:
            copy.wait_send()


def greet(peers):
    barrier = pltpu.get_barrier_semaphore()
    for peer in peers:
        pl.semaphore_signal(barrier, inc=1, device_id=peer, device_id_type=MESH)
    pl.semaphore_wait(barrier, len(peers))


def lanes(shape):
    return lax.broadcasted_iota(jnp.int32, shape, len(shape) - 1)


def wheel(table):
    lane = lanes(table.shape)
    twice = jnp.where(lane < 64, table, pltpu.roll(table, 64, 1))
    turned = pltpu.roll(twice, 32, 1)
    first = lax.rem(lane, 64) < 32
    return jnp.where(first, twice, turned), jnp.where(first, -turned, twice)


def turn(field, cosine, sine):
    first = lax.rem(lanes(field.shape), 64) < 32
    other = jnp.where(first, pltpu.roll(field, 96, 1), pltpu.roll(field, 32, 1))
    return field * cosine + other * sine


def key_masks(meta, table, f):
    query = table[:, 64:65]
    return [
        jnp.where(meta[f, pl.ds(j, 1), :] <= query, 0.0, -1e30).astype(F32) for j in range(8)
    ]


def forward_kernel(
    meta_in,
    table_in,
    tok_in,
    q_in,
    k_in,
    v_in,
    o_in,
    gate_in,
    up_in,
    down_in,
    dy_in,
    meta,
    table,
    tok,
    normed,
    queries,
    keys,
    logs,
    mixed,
    residual,
    normed_two,
    w_first,
    w_out,
    w_feed,
    w_down,
    dy,
    sums,
    got,
    mask,
    send_sems,
    recv_sems,
    local_sems,
):
    at = Spot()
    net = Copies(send_sems, recv_sems, local_sems)
    near = (1, 3, 2)
    slot = {1: 1, 3: 2, 2: 3}
    owner = {0: 0, 1: 3, 2: 1, 3: 2}
    greet(
        [at.fsdp(d) for d in range(1, 16)]
        + [at.to_y(d) for d in near]
        + [at.z_out(), at.z_hi()]
    )

    meta_copies = [net.send(meta_in, meta.at[at.f], at.fsdp(d)) for d in range(1, 16)]
    own_meta = net.local(meta_in, meta.at[at.f])
    tok_copies = [net.send(tok_in, tok.at[slot[d]], at.to_x(d)) for d in near]
    own_tok = net.local(tok_in, tok.at[0])
    table_copies = [net.send(table_in, table.at[slot[d]], at.to_x(d)) for d in near]
    own_table = net.local(table_in, table.at[0])

    def first_parts(d):
        rank = at.xs(d)
        half = rank // 2
        return (
            (q_in.at[:, pl.ds(pl.multiple_of(rank * 512, 128), 512)], pl.ds(0, 512)),
            (k_in.at[:, pl.ds(pl.multiple_of(half * 128, 128), 128)], pl.ds(512, 128)),
            (v_in.at[:, pl.ds(pl.multiple_of(half * 128, 128), 128)], pl.ds(640, 128)),
        )

    def feed_parts(d):
        rank = at.xs(d)
        span = pl.ds(pl.multiple_of(rank * 1408, 128), 1408)
        return ((gate_in.at[:, span], pl.ds(0, 1408)), (up_in.at[:, span], pl.ds(1408, 1408)))

    def spread(parts, full):
        mine = [net.local(s, full.at[at.x, at.z, at.c, :, t]) for s, t in parts(0)]
        away = {
            d: [net.send(s, full.at[at.x, at.z, at.c, :, t], at.to_x(d)) for s, t in parts(d)]
            for d in near
        }
        return mine, away

    def relay(full, d):
        x = at.xs(4 - d)
        block = full.at[x, at.z, at.c]
        z = net.send(block, block, at.z_in() if d in (0, 2) else at.z_out())
        return z, net.send(block, block, at.core())

    def relay_core(full, d):
        block = full.at[at.xs(4 - d), 1 - at.z, at.c]
        return net.send(block, block, at.core())

    first_mine, first_away = spread(first_parts, w_first)
    out_own = net.local(o_in, w_out.at[at.z, at.c])
    down_own = net.local(down_in, w_down.at[at.z, at.c])
    for copy in first_mine:
        copy.wait()
    first_hops = {0: relay(w_first, 0)}
    out_z = [
        net.send(o_in.at[pl.ds(0, 64)], w_out.at[at.z, at.c, pl.ds(0, 64)], at.z_in()),
        net.send(o_in.at[pl.ds(64, 64)], w_out.at[at.z, at.c, pl.ds(64, 64)], at.z_out()),
    ]
    out_c = [net.send(o_in, w_out.at[at.z, at.c], at.core())]
    feed_mine, feed_away = spread(feed_parts, w_feed)
    down_z = [
        net.send(down_in.at[pl.ds(0, 176)], w_down.at[at.z, at.c, pl.ds(0, 176)], at.z_in()),
        net.send(down_in.at[pl.ds(176, 176)], w_down.at[at.z, at.c, pl.ds(176, 176)], at.z_out()),
    ]
    down_c = [net.send(down_in, w_down.at[at.z, at.c], at.core())]
    for d in near:
        for copy in first_away[d]:
            copy.wait_recv()
        first_hops[d] = relay(w_first, d)
    first_last = []
    for d in (0, *near):
        first_hops[d][0].wait_recv()
        first_last.append(relay_core(w_first, d))
    for copy in feed_mine:
        copy.wait()
    feed_hops = {0: relay(w_feed, 0)}
    dy_copies = [net.send(dy_in, dy.at[slot[d]], at.to_x(d)) for d in near]
    own_dy = net.local(dy_in, dy.at[0])

    own_meta.wait()
    own_tok.wait()
    own_table.wait()
    for copy in (*meta_copies, *tok_copies, *table_copies):
        copy.wait_recv()
    for hop in first_hops.values():
        hop[1].wait_recv()
    for copy in first_last:
        copy.wait_recv()
    odd = lax.rem(at.x, 2) == 1

    def project(s, carry):
        values = tok[s].astype(F32)
        scale = lax.rsqrt(jnp.mean(values * values, axis=-1, keepdims=True) + epsilon)
        total = jnp.zeros((128, 768), F32)
        for f in range(16):
            span = pl.ds(f * 128, 128)
            normed[s, :, span] = (tok[s, :, span].astype(F32) * scale * meta[f, 8:9, :]).astype(BF)
        for g in range(8):
            total += dot(
                normed[s, :, pl.ds(g * 256, 256)],
                w_first[g // 2, g % 2].reshape(256, 768),
            )
        cosine, sine = wheel(table[s])
        for t in range(4):
            span = slice(t * 128, t * 128 + 128)
            queries[s, :, span] = (turn(total[:, span], cosine, sine) * 0.125).astype(BF)
        key, value = total[:, 512:640], total[:, 640:768]
        key = turn(jnp.where(odd, pltpu.roll(key, 64, 1), key), cosine, sine)
        value = jnp.where(odd, value, pltpu.roll(value, 64, 1))
        keys[s, at.ctx] = jnp.where(lanes((128, 128)) < 64, key, value).astype(BF)
        return carry

    lax.fori_loop(0, 4, project, 0)
    mine = keys.at[:, at.ctx]
    over = net.send(mine, mine, at.z_hi())
    key_copies = [net.send(mine, mine, at.to_y(d)) for d in near]
    for d in near:
        for copy in feed_away[d]:
            copy.wait_recv()
        feed_hops[d] = relay(w_feed, d)
    over.wait_recv()
    theirs = keys.at[:, (1 - at.hi) * 4 + at.y]
    key_copies += [net.send(theirs, theirs, at.to_y(d)) for d in near]
    out_own.wait()
    for copy in out_z:
        copy.wait_recv()
    out_c.append(net.send(w_out.at[1 - at.z, at.c], w_out.at[1 - at.z, at.c], at.core()))
    for copy in out_c:
        copy.wait_recv()
    for copy in key_copies:
        copy.wait_recv()

    def attend(s):
        masks = key_masks(meta, table[s], at.xs(owner[s]) * 4 + at.zc)
        for j in range(8):
            mask[:, j * 128 : j * 128 + 128] = masks[j]
        both = keys[s].reshape(1024, 128).astype(F32)
        lane = lanes(both.shape)
        key = jnp.where(lane < 64, both, 0.0)
        value = jnp.where(lane < 64, 0.0, both)
        key_pair = (key.astype(BF), pltpu.roll(key, 64, 1).astype(BF))
        value_pair = (pltpu.roll(value, 64, 1).astype(BF), value.astype(BF))
        head_lane = lanes((128, 128))
        log_rows = jnp.zeros((128, 128), F32)
        for t in range(4):
            query = queries[s, :, t * 128 : t * 128 + 128]
            total = jnp.zeros((128, 128), F32)
            for p in range(2):
                scores = dot_t(query, key_pair[p]) + mask[...]
                largest = jnp.max(scores, axis=-1, keepdims=True)
                weights = jnp.exp(scores - largest)
                amount = jnp.sum(weights, axis=-1, keepdims=True)
                total += dot(weights.astype(BF), value_pair[p]) * (1.0 / amount)
                log_rows = jnp.where(
                    head_lane == 2 * t + p, largest + jnp.log(amount), log_rows
                )
            mixed[s, :, t * 128 : t * 128 + 128] = total.astype(BF)
        logs[s] = log_rows
        return dot(mixed[s], w_out[...].reshape(512, 2048))

    sum_copies = []
    for s, d in ((3, 2), (1, 3), (2, 1)):
        sums[s - 1] = attend(s).astype(BF)
        sum_copies.append(net.send(sums.at[s - 1], got.at[s - 1], at.to_x(d)))
    own = attend(0)
    feed_last = []
    for d in (0, *near):
        feed_hops[d][0].wait_recv()
        feed_last.append(relay_core(w_feed, d))
    for copy in sum_copies:
        copy.wait_recv()
    total = tok[0].astype(F32) + own
    for i in range(3):
        total += got[i].astype(F32)
    residual[...] = total
    scale = lax.rsqrt(jnp.mean(total * total, axis=-1, keepdims=True) + epsilon)
    for f in range(16):
        span = pl.ds(f * 128, 128)
        normed_two[0, :, span] = (residual[:, span] * scale * meta[f, 9:10, :]).astype(BF)
    two_copies = [
        net.send(normed_two.at[0], normed_two.at[slot[d]], at.to_x(d)) for d in near
    ]
    down_own.wait()
    for copy in down_z:
        copy.wait_recv()
    down_c.append(net.send(w_down.at[1 - at.z, at.c], w_down.at[1 - at.z, at.c], at.core()))
    own_dy.wait()
    for hop in feed_hops.values():
        hop[1].wait_recv()
    for copy in (*down_c, *dy_copies, *feed_last, *two_copies):
        copy.wait_recv()
    net.finish()


def forward(meta, table, tok, q, k, v, o, gate, up, down, dy):
    shape = jax.ShapeDtypeStruct
    outs = (
        shape((16, 16, 128), F32),
        shape((4, 128, 128), F32),
        shape((4, 128, 2048), BF),
        shape((4, 128, 2048), BF),
        shape((4, 128, 512), BF),
        shape((4, 8, 128, 128), BF),
        shape((4, 128, 128), F32),
        shape((4, 128, 512), BF),
        shape((128, 2048), F32),
        shape((4, 128, 2048), BF),
        shape((4, 2, 2, 128, 768), BF),
        shape((2, 2, 128, 2048), BF),
        shape((4, 2, 2, 128, 2816), BF),
        shape((2, 2, 352, 2048), BF),
        shape((4, 128, 2048), BF),
    )
    return pl.pallas_call(
        forward_kernel,
        name="forward",
        out_shape=outs,
        in_specs=[EVERYWHERE] * 11,
        out_specs=(ON_CHIP,) * 12 + (EVERYWHERE,) * 3,
        scratch_shapes=[
            pltpu.VMEM((3, 128, 2048), BF),
            pltpu.VMEM((3, 128, 2048), BF),
            pltpu.VMEM((128, 1024), F32),
            pltpu.SemaphoreType.DMA((96,)),
            pltpu.SemaphoreType.DMA((96,)),
            pltpu.SemaphoreType.DMA((16,)),
        ],
        compiler_params=pltpu.CompilerParams(
            collective_id=1, has_side_effects=True, vmem_limit_bytes=VMEM_LIMIT
        ),
    )(meta, table, tok, q, k, v, o, gate, up, down, dy)


def per_device(
    tokens,
    positions,
    attention_gain,
    query_weight,
    key_weight,
    value_weight,
    out_weight,
    feed_gain,
    gate_weight,
    up_weight,
    down_weight,
    cotangent,
):
    at = Where()
    width = tokens.shape[3]
    heads = query_weight.shape[1] // HEAD_DIM // 4
    hidden = gate_weight.shape[1] // 4
    q_width = heads * HEAD_DIM

    places = positions.reshape(2, 8, 64).transpose(1, 0, 2).reshape(8, 128).astype(F32)
    meta = jnp.concatenate(
        [places, attention_gain[None], feed_gain[None], jnp.zeros((6, 128), F32)], axis=0
    )
    own_places = pick(places, at.ctx)[:, None]
    angles = own_places * frequencies(HEAD_DIM)[None]
    table = jnp.concatenate(
        [jnp.cos(angles), jnp.sin(angles), jnp.broadcast_to(own_places, (128, 64))], axis=1
    )
    token_rows = tokens.reshape(128, width)
    branch_grad = cotangent.reshape(128, width)
    (
        meta,
        table,
        _,
        normed,
        query_rot,
        keys,
        logs,
        mixed_low,
        residual,
        normed_two,
        w_first,
        w_out,
        w_feed,
        w_down,
        branch4,
    ) = forward(
        meta,
        table,
        token_rows,
        query_weight,
        key_weight,
        value_weight,
        out_weight,
        gate_weight,
        up_weight,
        down_weight,
        branch_grad,
    )
    gain_one = meta[:, 8].reshape(width)
    gain_two = meta[:, 9].reshape(width)
    normed = normed.reshape(512, width)
    normed_two = normed_two.reshape(512, width)
    branch4 = branch4.reshape(512, width)
    mixed_low = mixed_low.reshape(512, q_width)
    w_first = w_first.reshape(width, 768)
    full_out = w_out.reshape(q_width, width)
    w_feed = w_feed.reshape(width, 2 * hidden)
    full_down = w_down.reshape(hidden, width)
    cosine, sine_part = table[:, :, :32], table[:, :, 32:64]
    own_places = table[:, :, 64]
    zc = at.z * 2 + at.c
    key_places = jnp.stack(
        [pick(meta, cyc(at.x, d) * 4 + zc)[:8].reshape(1024) for d in (0, -1, 1, 2)]
    )
    pair = keys.reshape(4, 1024, 2 * HEAD_DIM)
    key_seq, value_seq = pair[..., :HEAD_DIM], pair[..., HEAD_DIM:]
    log_totals = logs[:, :, :heads].transpose(0, 2, 1)[..., None]
    hidden_in = token_rows.astype(F32)
    scale_one = lax.rsqrt(jnp.mean(hidden_in * hidden_in, axis=-1, keepdims=True) + epsilon)
    scale_two = lax.rsqrt(jnp.mean(residual * residual, axis=-1, keepdims=True) + epsilon)

    both = dot(normed_two, w_feed)
    gate, upward = both[:, :hidden], both[:, hidden:]
    sigmoid_gate = jax.nn.sigmoid(gate)
    activated = gate * sigmoid_gate
    product = (activated * upward).astype(BF)
    product_grad = dot_t(branch4, full_down)
    slope = sigmoid_gate * (1.0 + gate * (1.0 - sigmoid_gate))
    both_grad = jnp.concatenate(
        [
            (product_grad * upward * slope).astype(BF),
            (product_grad * activated).astype(BF),
        ],
        axis=1,
    )
    normed_two_grad = scatter_x(dot_t(both_grad, w_feed).reshape(4, 128, width))
    norm_two_back, gain_two_term = norm_backward(residual, scale_two, gain_two, normed_two_grad)
    residual_grad = branch_grad.astype(F32) + norm_two_back

    result = residual + scatter_x(dot(product, full_down).reshape(4, 128, width))
    output = result.astype(BF).reshape(tokens.shape)
    down_sum = row_grads(t_dot(product, branch4).astype(BF), at)
    both_sum = column_grads(t_dot(normed_two, both_grad).astype(BF), at).astype(F32)

    branch_low = gather_x(residual_grad.astype(BF))
    mixed_grad = dot_t(branch_low, full_out).astype(BF)
    out_sum = row_grads(t_dot(mixed_low, branch_low).astype(BF), at)
    query_grad, key_grad, value_grad = attend_backward(
        query_rot.reshape(4, 128, heads, HEAD_DIM),
        key_seq,
        value_seq,
        own_places,
        key_places,
        log_totals,
        mixed_grad.reshape(4, 128, heads, HEAD_DIM),
    )
    pair_grad = jnp.concatenate([key_grad, value_grad], axis=-1).reshape(4, 2, 4, 128, 2 * HEAD_DIM)
    pair_grad = pick(pair_grad, at.hi, 1), pick(pair_grad, 1 - at.hi, 1)
    pair_grad = jnp.stack(pair_grad)
    low = pair_grad.astype(BF)
    pair_grad = (
        pick(pair_grad, at.y, 2)
        + move(pick(low, cyc(at.y, 1), 2), Y_UP).astype(F32)
        + move(pick(low, cyc(at.y, -1), 2), Y_DOWN).astype(F32)
        + move(pick(low, cyc(at.y, 2), 2), Y_FAR).astype(F32)
    )
    pair_grad = pair_grad[0] + move(pair_grad[1].astype(BF), Z_HI).astype(F32)
    query_pre = rotate(query_grad, cosine[:, :, None], -sine_part[:, :, None]).astype(BF)
    key_pre = rotate(pair_grad[..., :HEAD_DIM], cosine, -sine_part).astype(BF).reshape(512, HEAD_DIM)
    value_pre = pair_grad[..., HEAD_DIM:].astype(BF).reshape(512, HEAD_DIM)
    query_pre = query_pre.reshape(512, q_width)
    pre = jnp.concatenate([query_pre, key_pre, value_pre], axis=1)
    odd = lax.rem(at.x, 2) == 1
    none = jnp.zeros_like(key_pre)
    window = lambda a: jnp.where(
        odd, jnp.concatenate([none, a], axis=1), jnp.concatenate([a, none], axis=1)
    )
    wide_pre = jnp.concatenate([query_pre, window(key_pre), window(value_pre)], axis=1)
    normed_grad = scatter_x(dot_t(wide_pre, w_first).reshape(4, 128, width))
    norm_one_back, gain_one_term = norm_backward(hidden_in, scale_one, gain_one, normed_grad)
    input_grad = residual_grad + norm_one_back
    first_sum = column_grads(t_dot(normed, pre).astype(BF), at).astype(F32)

    terms = jnp.stack([gain_one_term, gain_two_term])
    for pairs in (CORE, Z_IN, Z_HI, X_NEAR, X_FAR, Y_NEAR, Y_FAR):
        terms = terms + move(terms, pairs)
    terms = lax.dynamic_slice_in_dim(terms, at.fsdp * 128, 128, 1)
    return (
        output,
        input_grad.reshape(tokens.shape),
        terms[0],
        first_sum[:, :, :q_width].reshape(128, -1),
        first_sum[:, :, q_width : q_width + HEAD_DIM].reshape(128, -1),
        first_sum[:, :, q_width + HEAD_DIM :].reshape(128, -1),
        out_sum,
        terms[1],
        both_sum[:, :, :hidden].reshape(128, -1),
        both_sum[:, :, hidden:].reshape(128, -1),
        down_sum,
    )


def solution(mesh):
    rows = P("fsdp", None)
    blocks = P("fsdp", None, "ctx", None)
    return jax.shard_map(
        per_device,
        mesh=mesh,
        in_specs=(
            blocks,
            P("fsdp", None, None),
            P("fsdp"),
            rows,
            rows,
            rows,
            rows,
            P("fsdp"),
            rows,
            rows,
            rows,
            blocks,
        ),
        out_specs=(blocks, blocks, P("fsdp"), rows, rows, rows, rows, P("fsdp"), rows, rows, rows),
        check_vma=False,
    )
```

```python
import jax
import jax.numpy as jnp
from jax import lax
from jax.experimental import pallas as pl
from jax.experimental.pallas import tpu as pltpu
from jax.sharding import PartitionSpec as P

HEAD_DIM = 64
BF = jnp.bfloat16
F32 = jnp.float32
epsilon = 1e-05


def dot(a, b):
    return jnp.dot(a, b, preferred_element_type=F32)


def dot_t(a, b):
    return lax.dot_general(a, b, (((1,), (1,)), ((), ())), preferred_element_type=F32)


def t_dot(a, b):
    return lax.dot_general(a, b, (((0,), (0,)), ((), ())), preferred_element_type=F32)


def frequencies(head_width):
    return 10000.0 ** (-(2.0 * jnp.arange(head_width // 2, dtype=F32)) / head_width)


MESH = pl.DeviceIdType.MESH
EVERYWHERE = pl.BlockSpec(memory_space=pl.ANY)
ON_CHIP = pl.BlockSpec(memory_space=pltpu.VMEM)
VMEM_LIMIT = 62 * 2**20


class Spot:
    def __init__(self):
        ctx, f = lax.axis_index("ctx"), lax.axis_index("fsdp")
        self.ctx, self.f = ctx, f
        self.y, self.hi = lax.rem(ctx, 4), ctx // 4
        self.x, self.z, self.c = f // 4, lax.rem(f // 2, 2), lax.rem(f, 2)
        self.zc = lax.rem(f, 4)

    def xs(self, d):
        return lax.rem(self.x + d, 4)

    def ys(self, d):
        return lax.rem(self.y + d, 4)

    def to_x(self, d):
        return (self.ctx, self.xs(d) * 4 + self.zc)

    def to_y(self, d):
        return (self.hi * 4 + self.ys(d), self.f)

    def z_in(self):
        return (self.ctx, self.x * 4 + (1 - self.z) * 2 + self.c)

    def z_out(self):
        return ((1 - self.hi) * 4 + self.y, self.x * 4 + (1 - self.z) * 2 + self.c)

    def z_hi(self):
        return ((1 - self.hi) * 4 + self.y, self.f)

    def core(self):
        return (self.ctx, self.x * 4 + self.z * 2 + 1 - self.c)

    def fsdp(self, d):
        return (self.ctx, lax.rem(self.f + d, 16))


class Copies:
    def __init__(self, send_sems, recv_sems, local_sems):
        self.send_sems, self.recv_sems, self.local_sems = send_sems, recv_sems, local_sems
        self.count = self.local_count = 0
        self.started = []

    def send(self, source, target, peer):
        copy = pltpu.make_async_remote_copy(
            src_ref=source,
            dst_ref=target,
            send_sem=self.send_sems.at[self.count],
            recv_sem=self.recv_sems.at[self.count],
            device_id=peer,
            device_id_type=MESH,
        )
        self.count += 1
        copy.start()
        self.started.append(copy)
        return copy

    def local(self, source, target):
        copy = pltpu.make_async_copy(source, target, self.local_sems.at[self.local_count])
        self.local_count += 1
        copy.start()
        return copy

    def finish(self):
        for copy in self.started:
            copy.wait_send()


def greet(peers):
    barrier = pltpu.get_barrier_semaphore()
    for peer in peers:
        pl.semaphore_signal(barrier, inc=1, device_id=peer, device_id_type=MESH)
    pl.semaphore_wait(barrier, len(peers))


def lanes(shape):
    return lax.broadcasted_iota(jnp.int32, shape, len(shape) - 1)


def wheel(table):
    lane = lanes(table.shape)
    twice = jnp.where(lane < 64, table, pltpu.roll(table, 64, 1))
    turned = pltpu.roll(twice, 32, 1)
    first = lax.rem(lane, 64) < 32
    return jnp.where(first, twice, turned), jnp.where(first, -turned, twice)


def turn(field, cosine, sine):
    first = lax.rem(lanes(field.shape), 64) < 32
    other = jnp.where(first, pltpu.roll(field, 96, 1), pltpu.roll(field, 32, 1))
    return field * cosine + other * sine


def key_masks(meta, table, f):
    query = table[:, 64:65]
    return [
        jnp.where(meta[f, pl.ds(j, 1), :] <= query, 0.0, -1e30).astype(F32) for j in range(8)
    ]


def forward_kernel(
    meta_in,
    table_in,
    tok_in,
    q_in,
    k_in,
    v_in,
    o_in,
    gate_in,
    up_in,
    down_in,
    dy_in,
    meta,
    table,
    tok,
    normed,
    queries,
    keys,
    logs,
    mixed,
    residual,
    normed_two,
    w_first,
    w_out,
    w_feed,
    w_down,
    dy,
    sums,
    got,
    mask,
    send_sems,
    recv_sems,
    local_sems,
):
    at = Spot()
    net = Copies(send_sems, recv_sems, local_sems)
    near = (1, 3, 2)
    slot = {1: 1, 3: 2, 2: 3}
    owner = {0: 0, 1: 3, 2: 1, 3: 2}
    greet(
        [at.fsdp(d) for d in range(1, 16)]
        + [at.to_y(d) for d in near]
        + [at.z_out(), at.z_hi()]
    )

    meta_copies = [net.send(meta_in, meta.at[at.f], at.fsdp(d)) for d in range(1, 16)]
    own_meta = net.local(meta_in, meta.at[at.f])
    tok_copies = [net.send(tok_in, tok.at[slot[d]], at.to_x(d)) for d in near]
    own_tok = net.local(tok_in, tok.at[0])
    table_copies = [net.send(table_in, table.at[slot[d]], at.to_x(d)) for d in near]
    own_table = net.local(table_in, table.at[0])

    def first_parts(d):
        rank = at.xs(d)
        half = rank // 2
        return (
            (q_in.at[:, pl.ds(pl.multiple_of(rank * 512, 128), 512)], pl.ds(0, 512)),
            (k_in.at[:, pl.ds(pl.multiple_of(half * 128, 128), 128)], pl.ds(512, 128)),
            (v_in.at[:, pl.ds(pl.multiple_of(half * 128, 128), 128)], pl.ds(640, 128)),
        )

    def feed_parts(d):
        rank = at.xs(d)
        span = pl.ds(pl.multiple_of(rank * 1408, 128), 1408)
        return ((gate_in.at[:, span], pl.ds(0, 1408)), (up_in.at[:, span], pl.ds(1408, 1408)))

    def spread(parts, full):
        mine = [net.local(s, full.at[at.x, at.z, at.c, :, t]) for s, t in parts(0)]
        away = {
            d: [net.send(s, full.at[at.x, at.z, at.c, :, t], at.to_x(d)) for s, t in parts(d)]
            for d in near
        }
        return mine, away

    def relay(full, d):
        x = at.xs(4 - d)
        block = full.at[x, at.z, at.c]
        z = net.send(block, block, at.z_in() if d in (0, 2) else at.z_out())
        return z, net.send(block, block, at.core())

    def relay_core(full, d):
        block = full.at[at.xs(4 - d), 1 - at.z, at.c]
        return net.send(block, block, at.core())

    first_mine, first_away = spread(first_parts, w_first)
    out_own = net.local(o_in, w_out.at[at.z, at.c])
    down_own = net.local(down_in, w_down.at[at.z, at.c])
    for copy in first_mine:
        copy.wait()
    first_hops = {0: relay(w_first, 0)}
    out_z = [
        net.send(o_in.at[pl.ds(0, 64)], w_out.at[at.z, at.c, pl.ds(0, 64)], at.z_in()),
        net.send(o_in.at[pl.ds(64, 64)], w_out.at[at.z, at.c, pl.ds(64, 64)], at.z_out()),
    ]
    out_c = [net.send(o_in, w_out.at[at.z, at.c], at.core())]
    feed_mine, feed_away = spread(feed_parts, w_feed)
    down_z = [
        net.send(down_in.at[pl.ds(0, 176)], w_down.at[at.z, at.c, pl.ds(0, 176)], at.z_in()),
        net.send(down_in.at[pl.ds(176, 176)], w_down.at[at.z, at.c, pl.ds(176, 176)], at.z_out()),
    ]
    down_c = [net.send(down_in, w_down.at[at.z, at.c], at.core())]
    for d in near:
        for copy in first_away[d]:
            copy.wait_recv()
        first_hops[d] = relay(w_first, d)
    first_last = []
    for d in (0, *near):
        first_hops[d][0].wait_recv()
        first_last.append(relay_core(w_first, d))
    for copy in feed_mine:
        copy.wait()
    feed_hops = {0: relay(w_feed, 0)}
    dy_copies = [net.send(dy_in, dy.at[slot[d]], at.to_x(d)) for d in near]
    own_dy = net.local(dy_in, dy.at[0])

    own_meta.wait()
    own_tok.wait()
    own_table.wait()
    for copy in (*meta_copies, *tok_copies, *table_copies):
        copy.wait_recv()
    for hop in first_hops.values():
        hop[1].wait_recv()
    for copy in first_last:
        copy.wait_recv()
    odd = lax.rem(at.x, 2) == 1

    def project(s, carry):
        values = tok[s].astype(F32)
        scale = lax.rsqrt(jnp.mean(values * values, axis=-1, keepdims=True) + epsilon)
        total = jnp.zeros((128, 768), F32)
        for f in range(16):
            span = pl.ds(f * 128, 128)
            normed[s, :, span] = (tok[s, :, span].astype(F32) * scale * meta[f, 8:9, :]).astype(BF)
        for g in range(8):
            total += dot(
                normed[s, :, pl.ds(g * 256, 256)],
                w_first[g // 2, g % 2].reshape(256, 768),
            )
        cosine, sine = wheel(table[s])
        for t in range(4):
            span = slice(t * 128, t * 128 + 128)
            queries[s, :, span] = (turn(total[:, span], cosine, sine) * 0.125).astype(BF)
        key, value = total[:, 512:640], total[:, 640:768]
        key = turn(jnp.where(odd, pltpu.roll(key, 64, 1), key), cosine, sine)
        value = jnp.where(odd, value, pltpu.roll(value, 64, 1))
        keys[s, at.ctx] = jnp.where(lanes((128, 128)) < 64, key, value).astype(BF)
        return carry

    lax.fori_loop(0, 4, project, 0)
    mine = keys.at[:, at.ctx]
    over = net.send(mine, mine, at.z_hi())
    key_copies = [net.send(mine, mine, at.to_y(d)) for d in near]
    for d in near:
        for copy in feed_away[d]:
            copy.wait_recv()
        feed_hops[d] = relay(w_feed, d)
    over.wait_recv()
    theirs = keys.at[:, (1 - at.hi) * 4 + at.y]
    key_copies += [net.send(theirs, theirs, at.to_y(d)) for d in near]
    out_own.wait()
    for copy in out_z:
        copy.wait_recv()
    out_c.append(net.send(w_out.at[1 - at.z, at.c], w_out.at[1 - at.z, at.c], at.core()))
    for copy in out_c:
        copy.wait_recv()
    for copy in key_copies:
        copy.wait_recv()

    def attend(s):
        masks = key_masks(meta, table[s], at.xs(owner[s]) * 4 + at.zc)
        for j in range(8):
            mask[:, j * 128 : j * 128 + 128] = masks[j]
        both = keys[s].reshape(1024, 128).astype(F32)
        lane = lanes(both.shape)
        key = jnp.where(lane < 64, both, 0.0)
        value = jnp.where(lane < 64, 0.0, both)
        key_pair = (key.astype(BF), pltpu.roll(key, 64, 1).astype(BF))
        value_pair = (pltpu.roll(value, 64, 1).astype(BF), value.astype(BF))
        head_lane = lanes((128, 128))
        log_rows = jnp.zeros((128, 128), F32)
        for t in range(4):
            query = queries[s, :, t * 128 : t * 128 + 128]
            total = jnp.zeros((128, 128), F32)
            for p in range(2):
                scores = dot_t(query, key_pair[p]) + mask[...]
                largest = jnp.max(scores, axis=-1, keepdims=True)
                weights = jnp.exp(scores - largest)
                amount = jnp.sum(weights, axis=-1, keepdims=True)
                total += dot(weights.astype(BF), value_pair[p]) * (1.0 / amount)
                log_rows = jnp.where(
                    head_lane == 2 * t + p, largest + jnp.log(amount), log_rows
                )
            mixed[s, :, t * 128 : t * 128 + 128] = total.astype(BF)
        logs[s] = log_rows
        return dot(mixed[s], w_out[...].reshape(512, 2048))

    sum_copies = []
    for s, d in ((3, 2), (1, 3), (2, 1)):
        sums[s - 1] = attend(s).astype(BF)
        sum_copies.append(net.send(sums.at[s - 1], got.at[s - 1], at.to_x(d)))
    own = attend(0)
    feed_last = []
    for d in (0, *near):
        feed_hops[d][0].wait_recv()
        feed_last.append(relay_core(w_feed, d))
    for copy in sum_copies:
        copy.wait_recv()
    total = tok[0].astype(F32) + own
    for i in range(3):
        total += got[i].astype(F32)
    residual[...] = total
    scale = lax.rsqrt(jnp.mean(total * total, axis=-1, keepdims=True) + epsilon)
    for f in range(16):
        span = pl.ds(f * 128, 128)
        normed_two[0, :, span] = (residual[:, span] * scale * meta[f, 9:10, :]).astype(BF)
    two_copies = [
        net.send(normed_two.at[0], normed_two.at[slot[d]], at.to_x(d)) for d in near
    ]
    down_own.wait()
    for copy in down_z:
        copy.wait_recv()
    down_c.append(net.send(w_down.at[1 - at.z, at.c], w_down.at[1 - at.z, at.c], at.core()))
    own_dy.wait()
    for hop in feed_hops.values():
        hop[1].wait_recv()
    for copy in (*down_c, *dy_copies, *feed_last, *two_copies):
        copy.wait_recv()
    net.finish()


def forward(meta, table, tok, q, k, v, o, gate, up, down, dy):
    shape = jax.ShapeDtypeStruct
    outs = (
        shape((16, 16, 128), F32),
        shape((4, 128, 128), F32),
        shape((4, 128, 2048), BF),
        shape((4, 128, 2048), BF),
        shape((4, 128, 512), BF),
        shape((4, 8, 128, 128), BF),
        shape((4, 128, 128), F32),
        shape((4, 128, 512), BF),
        shape((128, 2048), F32),
        shape((4, 128, 2048), BF),
        shape((4, 2, 2, 128, 768), BF),
        shape((2, 2, 128, 2048), BF),
        shape((4, 2, 2, 128, 2816), BF),
        shape((2, 2, 352, 2048), BF),
        shape((4, 128, 2048), BF),
    )
    return pl.pallas_call(
        forward_kernel,
        name="forward",
        out_shape=outs,
        in_specs=[EVERYWHERE] * 11,
        out_specs=(ON_CHIP,) * 12 + (EVERYWHERE,) * 3,
        scratch_shapes=[
            pltpu.VMEM((3, 128, 2048), BF),
            pltpu.VMEM((3, 128, 2048), BF),
            pltpu.VMEM((128, 1024), F32),
            pltpu.SemaphoreType.DMA((96,)),
            pltpu.SemaphoreType.DMA((96,)),
            pltpu.SemaphoreType.DMA((16,)),
        ],
        compiler_params=pltpu.CompilerParams(
            collective_id=1, has_side_effects=True, vmem_limit_bytes=VMEM_LIMIT
        ),
    )(meta, table, tok, q, k, v, o, gate, up, down, dy)


CHUNKS = ((0, 512), (512, 512), (1024, 384))


def feed_kernel(
    n2,
    dy,
    residual,
    meta,
    feed_in,
    down_in,
    output,
    dr,
    dz,
    keep_feed,
    keep_down,
    gain_term,
    w_feed,
    w_down,
    hid,
    dgu,
    part_two,
    part_y,
    got_two,
    got_y,
    core_feed,
    core_down,
    gain,
    send_sems,
    recv_sems,
    local_sems,
):
    at = Spot()
    net = Copies(send_sems, recv_sems, local_sems)
    near = (1, 3, 2)
    slot = {1: 1, 3: 2, 2: 3}
    load_feed = [net.local(feed_in.at[x], w_feed.at[x]) for x in range(4)]
    load_down = net.local(down_in, w_down)
    greet([at.to_x(d) for d in near] + [at.z_in(), at.z_out(), at.core()])
    for f in range(16):
        gain[:, f * 128 : f * 128 + 128] = meta[f, 9:10, :]
    for copy in load_feed:
        copy.wait()
    load_down.wait()

    two_copies = []
    for first in (2, 0):
        rows = slice(first * 128, first * 128 + 256)
        tokens_here = n2[first : first + 2].reshape(256, 2048)
        cotangent_here = dy[first : first + 2].reshape(256, 2048)
        for start, size in CHUNKS:
            gate = jnp.zeros((256, size), F32)
            up = jnp.zeros((256, size), F32)
            for x in range(4):
                some = tokens_here[:, x * 512 : x * 512 + 512]
                gate += dot(some, w_feed[x, :, :, :, start : start + size].reshape(512, size))
                up += dot(
                    some,
                    w_feed[x, :, :, :, 1408 + start : 1408 + start + size].reshape(512, size),
                )
            dhid = dot_t(cotangent_here, w_down[start : start + size, :])
            sigmoid = 1.0 / (1.0 + jnp.exp(-gate))
            activated = gate * sigmoid
            hid[rows, start : start + size] = (activated * up).astype(BF)
            slope = sigmoid * (1.0 + gate * (1.0 - sigmoid))
            dgu[rows, start : start + size] = (dhid * up * slope).astype(BF)
            dgu[rows, 1408 + start : 1408 + start + size] = (dhid * activated).astype(BF)
        for x in range(4):
            span = slice(x * 512, x * 512 + 512)
            term = dot_t(dgu[rows, :], w_feed[x].reshape(512, 2816))
            part_two[first + 1, :, span] = term[128:].astype(BF)
            if first == 0:
                dr[:, span] = term[:128]
            else:
                part_two[first, :, span] = term[:128].astype(BF)
        for s, d in ((3, 2), (2, 1)) if first else ((1, 3),):
            two_copies.append(net.send(part_two.at[s], got_two.at[s - 1], at.to_x(d)))

    core_copies = []
    for x in range(4):
        some = n2[:, :, x * 512 : x * 512 + 512].reshape(512, 512)
        for start, size in ((0, 1408), (1408, 1408)):
            w_feed[x, :, :, :, start : start + size] = (
                t_dot(some, dgu[:, start : start + size])
                .astype(BF)
                .reshape(2, 2, 128, size)
            )
        core_copies.append(net.send(w_feed.at[x, :, 1 - at.c], core_feed.at[x], at.core()))
    y_copies = []
    for first in (2, 0):
        rows = slice(first * 128, first * 128 + 256)
        for j in range(4):
            span = slice(j * 512, j * 512 + 512)
            term = dot(hid[rows, :], w_down[:, span]).astype(BF)
            part_y[first, :, span] = term[:128]
            part_y[first + 1, :, span] = term[128:]

    for copy in two_copies:
        copy.wait_recv()
    grad = dr[...]
    for i in range(3):
        grad += got_two[i].astype(F32)
    values = residual[...]
    scale = lax.rsqrt(jnp.mean(values * values, axis=-1, keepdims=True) + epsilon)
    gain_term[...] = jnp.sum(grad * values * scale, axis=0, keepdims=True)
    weighted = grad * gain[...]
    inner = jnp.mean(weighted * values, axis=-1, keepdims=True)
    dr[...] = dy[0].astype(F32) + weighted * scale - values * (scale * scale * scale * inner)
    dz[0] = dr[...].astype(BF)
    dz_copies = [net.send(dz.at[0], dz.at[slot[d]], at.to_x(d)) for d in near]
    for s, d in ((3, 2), (1, 3), (2, 1)):
        y_copies.append(net.send(part_y.at[s], got_y.at[s - 1], at.to_x(d)))

    for start, size in CHUNKS:
        w_down[start : start + size, :] = t_dot(
            hid[:, start : start + size], dy[...].reshape(512, 2048)
        ).astype(BF)

    def down_rows(z, c):
        return pl.ds(pl.multiple_of((z * 2 + c) * 352, 16), 352)

    core_copies += [
        net.send(w_down.at[down_rows(z, 1 - at.c)], core_down.at[z], at.core()) for z in range(2)
    ]
    z_copies = []
    for x in range(4):
        core_copies[x].wait_recv()
        w_feed[x, 1 - at.z, at.c] = (
            w_feed[x, 1 - at.z, at.c].astype(F32) + core_feed[x, 1 - at.z].astype(F32)
        ).astype(BF)
        z_copies.append(
            net.send(
                w_feed.at[x, 1 - at.z, at.c],
                keep_feed.at[x],
                at.z_in() if x < 2 else at.z_out(),
            )
        )
    for z in range(2):
        core_copies[4 + z].wait_recv()
    away = down_rows(1 - at.z, at.c)
    w_down[away, :] = (
        w_down[away, :].astype(F32) + core_down[1 - at.z].astype(F32)
    ).astype(BF)
    for half, peer in ((0, at.z_in()), (176, at.z_out())):
        z_copies.append(
            net.send(
                w_down.at[pl.ds(pl.multiple_of(((1 - at.z) * 2 + at.c) * 352 + half, 16), 176)],
                keep_down.at[pl.ds(half, 176)],
                peer,
            )
        )
    for x in range(4):
        z_copies[x].wait_recv()
        keep_feed[x] = (
            keep_feed[x].astype(F32)
            + w_feed[x, at.z, at.c].astype(F32)
            + core_feed[x, at.z].astype(F32)
        ).astype(BF)
    for copy in z_copies[4:]:
        copy.wait_recv()
    here = down_rows(at.z, at.c)
    keep_down[...] = (
        keep_down[...].astype(F32) + w_down[here, :].astype(F32) + core_down[at.z].astype(F32)
    ).astype(BF)
    for copy in y_copies:
        copy.wait_recv()
    total = residual[...] + part_y[0].astype(F32)
    for i in range(3):
        total += got_y[i].astype(F32)
    output[...] = total.astype(BF)
    for copy in dz_copies:
        copy.wait_recv()
    net.finish()


def feed(n2, dy, residual, meta, w_feed, w_down):
    shape = jax.ShapeDtypeStruct
    return pl.pallas_call(
        feed_kernel,
        name="feed",
        out_shape=(
            shape((128, 2048), BF),
            shape((128, 2048), F32),
            shape((4, 128, 2048), BF),
            shape((4, 128, 2816), BF),
            shape((352, 2048), BF),
            shape((1, 2048), F32),
        ),
        in_specs=[ON_CHIP] * 4 + [EVERYWHERE] * 2,
        out_specs=(ON_CHIP,) * 6,
        scratch_shapes=[
            pltpu.VMEM((4, 2, 2, 128, 2816), BF),
            pltpu.VMEM((1408, 2048), BF),
            pltpu.VMEM((512, 1408), BF),
            pltpu.VMEM((512, 2816), BF),
            pltpu.VMEM((4, 128, 2048), BF),
            pltpu.VMEM((4, 128, 2048), BF),
            pltpu.VMEM((3, 128, 2048), BF),
            pltpu.VMEM((3, 128, 2048), BF),
            pltpu.VMEM((4, 2, 128, 2816), BF),
            pltpu.VMEM((2, 352, 2048), BF),
            pltpu.VMEM((1, 2048), F32),
            pltpu.SemaphoreType.DMA((32,)),
            pltpu.SemaphoreType.DMA((32,)),
            pltpu.SemaphoreType.DMA((8,)),
        ],
        compiler_params=pltpu.CompilerParams(
            collective_id=2, has_side_effects=True, vmem_limit_bytes=VMEM_LIMIT
        ),
    )(n2, dy, residual, meta, w_feed, w_down)


NEAR = (1, 3, 2)


class Sums:
    def __init__(self, at, net):
        self.at, self.net = at, net

    def columns(self, terms, span, got_y, mine, got_z, place, row):
        at, net = self.at, self.net

        def quarter(y):
            return pl.ds(pl.multiple_of(y * 32, 32), 32)

        own = quarter(at.y)
        copies = [
            net.send(terms.at[:, quarter(at.ys(d)), span], got_y.at[i, :, :, span], at.to_y(d))
            for i, d in enumerate(NEAR)
        ]
        yield
        for copy in copies:
            copy.wait_recv()
        for r in range(4):
            total = terms[r, own, span].astype(F32)
            for i in range(3):
                total += got_y[i, r, :, span].astype(F32)
            mine[r, :, span] = total.astype(BF)
        copy = net.send(mine.at[:, :, span], got_z.at[:, :, span], at.z_hi())
        yield
        copy.wait_recv()
        for r in range(4):
            got_z[r, :, span] = (
                got_z[r, :, span].astype(F32) + mine[r, :, span].astype(F32)
            ).astype(BF)
        here = net.local(got_z.at[at.x, :, span], place(at.x))
        copies = [
            net.send(got_z.at[at.xs(d), :, span], place(at.x), at.to_x(d)) for d in NEAR
        ]
        here.wait()
        yield
        for copy in copies:
            copy.wait_recv()
        copies = [net.send(row, row, at.to_y(d)) for d in NEAR]
        yield
        for copy in copies:
            copy.wait_recv()

    def rows(self, terms, got_y, mine, got_z, out):
        at, net = self.at, self.net

        def quarter(y):
            return pl.ds(pl.multiple_of(y * 512, 128), 512)

        own = quarter(at.y)
        copies = [
            net.send(terms.at[:, quarter(at.ys(d))], got_y.at[i], at.to_y(d))
            for i, d in enumerate(NEAR)
        ]
        yield
        for copy in copies:
            copy.wait_recv()
        total = terms[:, own].astype(F32)
        for i in range(3):
            total += got_y[i].astype(F32)
        mine[...] = total.astype(BF)
        copy = net.send(mine, got_z, at.z_hi())
        yield
        copy.wait_recv()
        got_z[...] = (got_z[...].astype(F32) + mine[...].astype(F32)).astype(BF)
        here = net.local(got_z, out.at[:, own])
        copies = [net.send(got_z, out.at[:, own], at.to_y(d)) for d in NEAR]
        here.wait()
        yield
        for copy in copies:
            copy.wait_recv()

    def first(self, terms, span, got_core, got_z):
        at, net = self.at, self.net
        copy = net.send(
            terms.at[:, :, 1 - at.c, :, span], got_core.at[:, :, :, span], at.core()
        )
        yield
        copy.wait_recv()
        for r in range(4):
            terms[r, 1 - at.z, at.c, :, span] = (
                terms[r, 1 - at.z, at.c, :, span].astype(F32)
                + got_core[r, 1 - at.z, :, span].astype(F32)
            ).astype(BF)
        copies = [
            net.send(
                terms.at[r : r + 2, 1 - at.z, at.c, :, span], got_z.at[r : r + 2, :, span], peer
            )
            for r, peer in ((0, at.z_in()), (2, at.z_out()))
        ]
        yield
        for copy in copies:
            copy.wait_recv()
        for r in range(4):
            got_z[r, :, span] = (
                got_z[r, :, span].astype(F32)
                + terms[r, at.z, at.c, :, span].astype(F32)
                + got_core[r, at.z, :, span].astype(F32)
            ).astype(BF)

    def out(self, terms, got_core, got_z):
        at, net = self.at, self.net
        copy = net.send(terms.at[:, 1 - at.c], got_core, at.core())
        yield
        copy.wait_recv()
        terms[1 - at.z, at.c] = (
            terms[1 - at.z, at.c].astype(F32) + got_core[1 - at.z].astype(F32)
        ).astype(BF)
        copies = [
            net.send(
                terms.at[1 - at.z, at.c, pl.ds(r, 64)], got_z.at[pl.ds(r, 64)], peer
            )
            for r, peer in ((0, at.z_in()), (64, at.z_out()))
        ]
        yield
        for copy in copies:
            copy.wait_recv()
        got_z[...] = (
            got_z[...].astype(F32)
            + terms[at.z, at.c].astype(F32)
            + got_core[at.z].astype(F32)
        ).astype(BF)


def chained(*parts):
    for part in parts:
        yield from part


def backward_kernel(
    dz,
    dr,
    tok,
    meta,
    table,
    queries,
    keys,
    logs,
    mixed,
    normed,
    w_first,
    w_out,
    feed_terms,
    down_terms,
    gain_two,
    dx,
    gains,
    gate_sum,
    up_sum,
    down_sum,
    out_sum,
    first_sum,
    dmix,
    mask,
    probs,
    scores_grad,
    pre,
    key_part,
    key_got,
    part,
    got_part,
    out_terms,
    out_core,
    out_z,
    first_terms,
    first_core,
    first_z,
    feed_y,
    feed_mine,
    feed_z,
    down_y,
    down_mine,
    down_z,
    out_y,
    out_mine,
    out_zz,
    first_y,
    first_mine,
    first_zz,
    gain,
    gain_send,
    gain_got,
    gain_part,
    gain_last,
    send_sems,
    recv_sems,
    local_sems,
):
    at = Spot()
    net = Copies(send_sems, recv_sems, local_sems)
    slot = {1: 1, 3: 2, 2: 3}
    owner = {0: 0, 1: 3, 2: 1, 3: 2}

    def to_ctx(k):
        return (lax.rem(at.ctx + k, 8), at.f)

    greet(
        [at.fsdp(d) for d in range(1, 16)] + [to_ctx(k) for k in range(1, 8)] + [at.z_out()]
    )
    sums = Sums(at, net)
    own_rows = pl.ds(pl.multiple_of(at.y * 32, 32), 32)

    def rank_columns(r):
        return pl.ds(pl.multiple_of(r * 1408, 128), 1408)

    gate_chain = sums.columns(
        feed_terms,
        slice(0, 1408),
        feed_y,
        feed_mine,
        feed_z,
        lambda r: gate_sum.at[own_rows, rank_columns(r)],
        gate_sum.at[own_rows],
    )
    up_chain = sums.columns(
        feed_terms,
        slice(1408, 2816),
        feed_y,
        feed_mine,
        feed_z,
        lambda r: up_sum.at[own_rows, rank_columns(r)],
        up_sum.at[own_rows],
    )
    down_chain = sums.rows(down_terms, down_y, down_mine, down_z, down_sum)
    out_chain = chained(
        sums.out(out_terms, out_core, out_z), sums.rows(out_z, out_y, out_mine, out_zz, out_sum)
    )

    def first_chain(span):
        return chained(
            sums.first(first_terms, span, first_core, first_z),
            sums.columns(
                first_z,
                span,
                first_y,
                first_mine,
                first_zz,
                lambda r: first_sum.at[r, own_rows, span],
                first_sum.at[:, own_rows, span],
            ),
        )

    query_chain = first_chain(slice(0, 512))
    key_chain = first_chain(slice(512, 640))

    def step(*chains):
        for chain in chains:
            next(chain, None)

    step(gate_chain, up_chain)
    for f in range(16):
        gain[:, f * 128 : f * 128 + 128] = meta[f, 8:9, :]
    weight = w_out[...].reshape(512, 2048)
    for s in range(4):
        dmix[s] = dot_t(dz[s], weight).astype(BF)
    for j in range(2):
        span = slice(j * 1024, j * 1024 + 1024)
        out_terms[:, :, :, span] = (
            t_dot(mixed[...].reshape(512, 512), dz[:, :, span].reshape(512, 1024))
            .astype(BF)
            .reshape(2, 2, 128, 1024)
        )
    step(out_chain, down_chain)

    def attend(s):
        masks = key_masks(meta, table[s], at.xs(owner[s]) * 4 + at.zc)
        for j in range(8):
            mask[:, j * 128 : j * 128 + 128] = masks[j]
        both = keys[s].reshape(1024, 128).astype(F32)
        lane = lanes(both.shape)
        key = jnp.where(lane < 64, both, 0.0)
        value = jnp.where(lane < 64, 0.0, both)
        key_pair = (key.astype(BF), pltpu.roll(key, 64, 1).astype(BF))
        value_pair = (pltpu.roll(value, 64, 1).astype(BF), value.astype(BF))
        cosine, sine = wheel(table[s])
        for t in range(4):
            span = slice(t * 128, t * 128 + 128)
            query, grad = queries[s, :, span], dmix[s, :, span]
            total = jnp.zeros((128, 128), F32)
            for p in range(2):
                scores = dot_t(query, key_pair[p]) + mask[...]
                prob = jnp.exp(scores - logs[s, :, 2 * t + p : 2 * t + p + 1])
                prob_grad = dot_t(grad, value_pair[p])
                inner = jnp.sum(prob * prob_grad, axis=-1, keepdims=True)
                low = (prob * (prob_grad - inner)).astype(BF)
                probs[p, span, :] = prob.astype(BF)
                scores_grad[p, span, :] = low
                total += dot(low, key_pair[p])
            pre[s, :, span] = turn(total * 0.125, cosine, -sine).astype(BF)
        stack = lambda a: jnp.concatenate([a[s, :, t * 128 : t * 128 + 128] for t in range(4)], axis=0)
        query, grad = stack(queries), stack(dmix)
        half = lanes((1024, 128)) < 64
        key_grad = t_dot(scores_grad[0], query), t_dot(scores_grad[1], query)
        value_grad = t_dot(probs[0], grad), t_dot(probs[1], grad)
        total = jnp.where(
            half,
            key_grad[0] + pltpu.roll(key_grad[1], 64, 1),
            pltpu.roll(value_grad[0], 64, 1) + value_grad[1],
        )
        for j in range(8):
            key_part[j, s] = total[j * 128 : j * 128 + 128].astype(BF)

    def send_keys(first):
        return [
            net.send(
                key_part.at[lax.rem(at.ctx + k, 8), first : first + 2],
                key_got.at[k - 1, first : first + 2],
                to_ctx(k),
            )
            for k in range(1, 8)
        ]

    attend(0)
    step(out_chain)
    attend(1)
    key_copies = send_keys(0)
    step(out_chain)
    attend(2)
    step(gate_chain)
    attend(3)
    key_copies += send_keys(2)
    for x in range(4):
        first_terms[x, :, :, :, 0:512] = (
            t_dot(
                normed[:, :, x * 512 : x * 512 + 512].reshape(512, 512),
                pre[:, :, 0:512].reshape(512, 512),
            )
            .astype(BF)
            .reshape(2, 2, 128, 512)
        )
    step(query_chain, up_chain, down_chain, gate_chain, query_chain)
    for copy in key_copies:
        copy.wait_recv()
    odd = lax.rem(at.x, 2) == 1
    half = lanes((128, 128)) < 64
    windows = []
    for s in range(4):
        total = key_part[at.ctx, s].astype(F32)
        for k in range(7):
            total += key_got[k, s].astype(F32)
        cosine, sine = wheel(table[s])
        total = jnp.where(half, turn(total, cosine, -sine), total)
        pre[s, :, 512:640] = total.astype(BF)
        moved = pltpu.roll(total, 64, 1)
        windows.append(
            jnp.concatenate(
                [
                    jnp.where(half, jnp.where(odd, 0.0, total), jnp.where(odd, moved, 0.0)),
                    jnp.where(half, jnp.where(odd, 0.0, moved), jnp.where(odd, total, 0.0)),
                ],
                axis=1,
            ).astype(BF)
        )
    window = jnp.concatenate(windows, axis=0)
    for x in range(4):
        span = slice(x * 512, x * 512 + 512)
        term = dot_t(
            pre[:, :, 0:512].reshape(512, 512), w_first[x, :, :, :, 0:512].reshape(512, 512)
        ) + dot_t(window, w_first[x, :, :, :, 512:768].reshape(512, 256))
        dx[:, span] = term[:128]
        for s in range(1, 4):
            part[s, :, span] = term[s * 128 : s * 128 + 128].astype(BF)
    part_copies = [
        net.send(part.at[s], got_part.at[s - 1], at.to_x(d)) for s, d in ((3, 2), (1, 3), (2, 1))
    ]
    for x in range(4):
        first_terms[x, :, :, :, 512:640] = (
            t_dot(
                normed[:, :, x * 512 : x * 512 + 512].reshape(512, 512),
                pre[:, :, 512:640].reshape(512, 128),
            )
            .astype(BF)
            .reshape(2, 2, 128, 128)
        )
    step(key_chain, query_chain, key_chain, up_chain, out_chain)
    for copy in part_copies:
        copy.wait_recv()
    grad = dx[...]
    for i in range(3):
        grad += got_part[i].astype(F32)
    values = tok[...].astype(F32)
    scale = lax.rsqrt(jnp.mean(values * values, axis=-1, keepdims=True) + epsilon)
    gain_one = jnp.sum(grad * values * scale, axis=0, keepdims=True)
    weighted = grad * gain[...]
    inner = jnp.mean(weighted * values, axis=-1, keepdims=True)
    dx[...] = dr[...] + weighted * scale - values * (scale * scale * scale * inner)
    for f in range(16):
        span = slice(f * 128, f * 128 + 128)
        gain_send[f] = jnp.concatenate(
            [gain_one[:, span], gain_two[:, span], jnp.zeros((6, 128), F32)], axis=0
        )
    gain_copies = [
        net.send(gain_send.at[lax.rem(at.f + d, 16)], gain_got.at[d - 1], at.fsdp(d))
        for d in range(1, 16)
    ]
    step(key_chain, query_chain, gate_chain, down_chain, up_chain)
    for copy in gain_copies:
        copy.wait_recv()
    total = gain_send[at.f]
    for d in range(15):
        total += gain_got[d]
    gain_part[...] = total
    last_copies = [net.send(gain_part, gain_last.at[k - 1], to_ctx(k)) for k in range(1, 8)]
    step(key_chain, query_chain, out_chain)
    for _ in range(3):
        step(key_chain, query_chain, gate_chain, up_chain, down_chain, out_chain)
    for copy in last_copies:
        copy.wait_recv()
    total = gain_part[...]
    for k in range(7):
        total += gain_last[k]
    gains[...] = total
    for chain in (key_chain, query_chain, gate_chain, up_chain, down_chain, out_chain):
        for _ in chain:
            pass
    net.finish()


def backward(*operands):
    shape = jax.ShapeDtypeStruct
    vmem = lambda *dims: pltpu.VMEM(dims, BF)
    wide = lambda *dims: pltpu.VMEM(dims, F32)
    return pl.pallas_call(
        backward_kernel,
        name="backward",
        out_shape=(
            shape((128, 2048), F32),
            shape((8, 128), F32),
            shape((128, 5632), BF),
            shape((128, 5632), BF),
            shape((352, 2048), BF),
            shape((128, 2048), BF),
            shape((4, 128, 640), BF),
        ),
        in_specs=[ON_CHIP] * 15,
        out_specs=(ON_CHIP,) * 7,
        scratch_shapes=[
            vmem(4, 128, 512),
            wide(128, 1024),
            vmem(2, 512, 1024),
            vmem(2, 512, 1024),
            vmem(4, 128, 640),
            vmem(8, 4, 128, 128),
            vmem(7, 4, 128, 128),
            vmem(4, 128, 2048),
            vmem(3, 128, 2048),
            vmem(2, 2, 128, 2048),
            vmem(2, 128, 2048),
            vmem(128, 2048),
            vmem(4, 2, 2, 128, 640),
            vmem(4, 2, 128, 640),
            vmem(4, 128, 640),
            vmem(3, 4, 32, 2816),
            vmem(4, 32, 2816),
            vmem(4, 32, 2816),
            vmem(3, 352, 512),
            vmem(352, 512),
            vmem(352, 512),
            vmem(3, 128, 512),
            vmem(128, 512),
            vmem(128, 512),
            vmem(3, 4, 32, 640),
            vmem(4, 32, 640),
            vmem(4, 32, 640),
            wide(1, 2048),
            wide(16, 8, 128),
            wide(15, 8, 128),
            wide(8, 128),
            wide(7, 8, 128),
            pltpu.SemaphoreType.DMA((112,)),
            pltpu.SemaphoreType.DMA((112,)),
            pltpu.SemaphoreType.DMA((8,)),
        ],
        compiler_params=pltpu.CompilerParams(
            collective_id=3, has_side_effects=True, vmem_limit_bytes=VMEM_LIMIT
        ),
    )(*operands)


def per_device(
    tokens,
    positions,
    attention_gain,
    query_weight,
    key_weight,
    value_weight,
    out_weight,
    feed_gain,
    gate_weight,
    up_weight,
    down_weight,
    cotangent,
):
    width = tokens.shape[3]
    places = positions.reshape(2, 8, 64).transpose(1, 0, 2).reshape(8, 128).astype(F32)
    meta = jnp.concatenate(
        [places, attention_gain[None], feed_gain[None], jnp.zeros((6, 128), F32)], axis=0
    )
    own_places = lax.dynamic_index_in_dim(places, lax.axis_index("ctx"), 0, keepdims=False)[:, None]
    angles = own_places * frequencies(HEAD_DIM)[None]
    table = jnp.concatenate(
        [jnp.cos(angles), jnp.sin(angles), jnp.broadcast_to(own_places, (128, 64))], axis=1
    )
    token_rows = tokens.reshape(128, width)
    branch_grad = cotangent.reshape(128, width)
    (
        meta,
        table,
        _,
        normed,
        query_rot,
        keys,
        logs,
        mixed_low,
        residual,
        normed_two,
        w_first,
        w_out,
        w_feed,
        w_down,
        branch4,
    ) = forward(
        meta,
        table,
        token_rows,
        query_weight,
        key_weight,
        value_weight,
        out_weight,
        gate_weight,
        up_weight,
        down_weight,
        branch_grad,
    )
    output, residual_grad, branch_low, feed_terms, down_terms, gain_two_term = feed(
        normed_two, branch4, residual, meta, w_feed, w_down.reshape(1408, width)
    )
    input_grad, gains, gate_sum, up_sum, down_sum, out_sum, first_sum = backward(
        branch_low,
        residual_grad,
        token_rows,
        meta,
        table,
        query_rot,
        keys,
        logs,
        mixed_low,
        normed,
        w_first,
        w_out,
        feed_terms,
        down_terms,
        gain_two_term,
    )
    first_sum = first_sum.transpose(1, 0, 2).astype(F32)
    return (
        output.reshape(tokens.shape),
        input_grad.reshape(tokens.shape),
        gains[0],
        first_sum[:, :, :512].reshape(128, -1),
        first_sum[:, :, 512:576].reshape(128, -1),
        first_sum[:, :, 576:].reshape(128, -1),
        out_sum.astype(F32),
        gains[1],
        gate_sum.astype(F32),
        up_sum.astype(F32),
        down_sum.astype(F32),
    )


def solution(mesh):
    rows = P("fsdp", None)
    blocks = P("fsdp", None, "ctx", None)
    return jax.shard_map(
        per_device,
        mesh=mesh,
        in_specs=(
            blocks,
            P("fsdp", None, None),
            P("fsdp"),
            rows,
            rows,
            rows,
            rows,
            P("fsdp"),
            rows,
            rows,
            rows,
            blocks,
        ),
        out_specs=(blocks, blocks, P("fsdp"), rows, rows, rows, rows, P("fsdp"), rows, rows, rows),
        check_vma=False,
    )
```

```python
import jax
import jax.numpy as jnp
from jax import lax
from jax.experimental import pallas as pl
from jax.experimental.pallas import tpu as pltpu
from jax.sharding import PartitionSpec as P

HEAD_DIM = 64
BF = jnp.bfloat16
F32 = jnp.float32
epsilon = 1e-05


def dot(a, b):
    return jnp.dot(a, b, preferred_element_type=F32)


def dot_t(a, b):
    return lax.dot_general(a, b, (((1,), (1,)), ((), ())), preferred_element_type=F32)


def t_dot(a, b):
    return lax.dot_general(a, b, (((0,), (0,)), ((), ())), preferred_element_type=F32)


def frequencies(head_width):
    return 10000.0 ** (-(2.0 * jnp.arange(head_width // 2, dtype=F32)) / head_width)


MESH = pl.DeviceIdType.MESH
EVERYWHERE = pl.BlockSpec(memory_space=pl.ANY)
ON_CHIP = pl.BlockSpec(memory_space=pltpu.VMEM)
VMEM_LIMIT = 62 * 2**20


class Spot:
    def __init__(self):
        ctx, f = lax.axis_index("ctx"), lax.axis_index("fsdp")
        self.ctx, self.f = ctx, f
        self.y, self.hi = lax.rem(ctx, 4), ctx // 4
        self.x, self.z, self.c = f // 4, lax.rem(f // 2, 2), lax.rem(f, 2)
        self.zc = lax.rem(f, 4)

    def xs(self, d):
        return lax.rem(self.x + d, 4)

    def ys(self, d):
        return lax.rem(self.y + d, 4)

    def to_x(self, d):
        return (self.ctx, self.xs(d) * 4 + self.zc)

    def to_y(self, d):
        return (self.hi * 4 + self.ys(d), self.f)

    def z_in(self):
        return (self.ctx, self.x * 4 + (1 - self.z) * 2 + self.c)

    def z_out(self):
        return ((1 - self.hi) * 4 + self.y, self.x * 4 + (1 - self.z) * 2 + self.c)

    def z_hi(self):
        return ((1 - self.hi) * 4 + self.y, self.f)

    def core(self):
        return (self.ctx, self.x * 4 + self.z * 2 + 1 - self.c)

    def fsdp(self, d):
        return (self.ctx, lax.rem(self.f + d, 16))


class Copies:
    def __init__(self, send_sems, recv_sems, local_sems):
        self.send_sems, self.recv_sems, self.local_sems = send_sems, recv_sems, local_sems
        self.count = self.local_count = 0
        self.started = []

    def send(self, source, target, peer):
        copy = pltpu.make_async_remote_copy(
            src_ref=source,
            dst_ref=target,
            send_sem=self.send_sems.at[self.count],
            recv_sem=self.recv_sems.at[self.count],
            device_id=peer,
            device_id_type=MESH,
        )
        self.count += 1
        copy.start()
        self.started.append(copy)
        return copy

    def local(self, source, target):
        copy = pltpu.make_async_copy(source, target, self.local_sems.at[self.local_count])
        self.local_count += 1
        copy.start()
        return copy

    def finish(self):
        for copy in self.started:
            copy.wait_send()


class Ring:
    def __init__(self, at, net, own, slots):
        self.at, self.net, self.slots = at, net, slots
        self.up = net.send(own, slots.at[1], at.to_x(1))
        self.down = net.send(own, slots.at[2], at.to_x(3))
        self.far = []

    def forward(self):
        at, net, slots = self.at, self.net, self.slots
        half = slots.shape[1] // 2
        for copy, s, start, peer in (
            (self.up, 1, 0, at.to_x(1)),
            (self.down, 2, half, at.to_x(3)),
        ):
            copy.wait_recv()
            rows = pl.ds(start, half)
            self.far.append(net.send(slots.at[s, rows], slots.at[3, rows], peer))

    def wait(self):
        for copy in self.far:
            copy.wait_recv()


def greet(peers):
    barrier = pltpu.get_barrier_semaphore()
    for peer in peers:
        pl.semaphore_signal(barrier, inc=1, device_id=peer, device_id_type=MESH)
    pl.semaphore_wait(barrier, len(peers))


def lanes(shape):
    return lax.broadcasted_iota(jnp.int32, shape, len(shape) - 1)


def wheel(table):
    lane = lanes(table.shape)
    other = pltpu.roll(table, 64, 1)
    twice = jnp.concatenate(
        [jnp.where(lane < 64, table, other), jnp.where(lane < 64, other, table)], axis=0
    )
    turned = pltpu.roll(twice, 32, 1)
    first = lax.rem(lanes(twice.shape), 64) < 32
    return jnp.where(first, twice, turned), jnp.where(first, -turned, twice)


def turn(field, cosine, sine):
    first = lax.rem(lanes(field.shape), 64) < 32
    other = jnp.where(first, pltpu.roll(field, 96, 1), pltpu.roll(field, 32, 1))
    return field * cosine + other * sine


def key_masks(meta, f, ctx):
    own = meta[f, pl.ds(ctx, 1), :]
    diagonal = lax.broadcasted_iota(jnp.int32, (128, 128), 0) == lanes((128, 128))
    query = jnp.sum(jnp.where(diagonal, own, 0.0), axis=1, keepdims=True)
    return [
        jnp.where(meta[f, pl.ds(j, 1), :] <= query, 0.0, -1e30).astype(F32) for j in range(8)
    ]


def forward_kernel(
    meta_in,
    table_in,
    tok_in,
    q_in,
    k_in,
    v_in,
    o_in,
    gate_in,
    up_in,
    down_in,
    dy_in,
    meta,
    table,
    tok,
    normed,
    queries,
    keys,
    logs,
    mixed,
    residual,
    normed_two,
    w_first,
    w_out,
    w_feed,
    w_down,
    dy,
    sums,
    got,
    mask,
    stage_feed,
    stage_down,
    stage_dy,
    send_sems,
    recv_sems,
    local_sems,
):
    at = Spot()
    net = Copies(send_sems, recv_sems, local_sems)
    near = (1, 3, 2)
    slot = {1: 1, 3: 2, 2: 3}
    owner = {0: 0, 1: 3, 2: 1, 3: 2}
    greet(
        [at.fsdp(d) for d in range(1, 16)]
        + [at.to_y(d) for d in near]
        + [at.z_out(), at.z_hi()]
    )

    quarter = pl.ds(pl.multiple_of(at.y * 32, 32), 32)

    def first_parts(d, rows):
        rank = at.xs(d)
        half = pl.ds(pl.multiple_of(rank // 2 * 128, 128), 128)
        return (
            (q_in.at[rows, pl.ds(pl.multiple_of(rank * 512, 128), 512)], pl.ds(0, 512)),
            (k_in.at[rows, half], pl.ds(512, 128)),
            (v_in.at[rows, half], pl.ds(640, 128)),
        )

    def feed_parts(d, rows):
        span = pl.ds(pl.multiple_of(at.xs(d) * 1408, 128), 1408)
        return (
            (gate_in.at[rows, span], pl.ds(0, 1408)),
            (up_in.at[rows, span], pl.ds(1408, 1408)),
        )

    everything = pl.ds(0, 128)

    def spread(parts, full, stage):
        mine = [net.local(s, stage.at[:, t]) for s, t in parts(0, everything)]
        away = {
            d: [
                net.send(s, full.at[at.x, at.z, at.c, quarter, t], at.to_x(d))
                for s, t in parts(d, quarter)
            ]
            for d in near
        }
        return mine, away

    def share(full, away, d):
        for copy in away[d]:
            copy.wait_recv()
        block = full.at[at.xs(4 - d), at.z, at.c, quarter]
        return [net.send(block, block, at.to_y(e)) for e in near]

    def relay(full, d, source=None):
        block = full.at[at.xs(4 - d), at.z, at.c]
        source = block if source is None else source
        z = net.send(source, block, at.z_in() if d in (0, 2) else at.z_out())
        return z, net.send(source, block, at.core())

    def relay_core(full, d):
        block = full.at[at.xs(4 - d), 1 - at.z, at.c]
        return net.send(block, block, at.core())

    own_first = w_first.at[at.x, at.z, at.c]
    first_mine, first_away = spread(first_parts, w_first, own_first)
    tok_ring = Ring(at, net, tok_in, tok)
    own_tok = net.local(tok_in, tok.at[0])
    meta_copies = [net.send(meta_in, meta.at[at.f], at.fsdp(d)) for d in range(1, 16)]
    own_meta = net.local(meta_in, meta.at[at.f])
    table_copies = [net.send(table_in, table.at[slot[d]], at.to_x(d)) for d in near]
    own_table = net.local(table_in, table.at[0])
    for copy in first_mine:
        copy.wait()
    first_hops = {0: relay(w_first, 0)}
    first_shared = {d: share(w_first, first_away, d) for d in near}
    feed_mine, feed_away = spread(feed_parts, w_feed, stage_feed)
    own_out = net.local(o_in, w_out.at[at.z, at.c])
    load_down = net.local(down_in, stage_down)
    load_dy = net.local(dy_in, stage_dy)
    out_z = [
        net.send(o_in.at[pl.ds(0, 64)], w_out.at[at.z, at.c, pl.ds(0, 64)], at.z_in()),
        net.send(o_in.at[pl.ds(64, 64)], w_out.at[at.z, at.c, pl.ds(64, 64)], at.z_out()),
    ]
    out_c = [net.send(o_in, w_out.at[at.z, at.c], at.core())]
    for d in near:
        for copy in first_shared[d]:
            copy.wait_recv()
        first_hops[d] = relay(w_first, d)
    for copy in feed_mine:
        copy.wait()
    store = [net.local(stage_feed, w_feed.at[at.x, at.z, at.c])]
    feed_hops = {0: relay(w_feed, 0, stage_feed)}
    tok_ring.forward()
    dy_ring = Ring(at, net, dy_in, dy)
    load_down.wait()
    load_dy.wait()
    store.append(net.local(stage_down, w_down.at[at.z, at.c]))
    store.append(net.local(stage_dy, dy.at[0]))
    first_last = []
    for d in (0, *near):
        first_hops[d][0].wait_recv()
        first_last.append(relay_core(w_first, d))
    feed_shared = {d: share(w_feed, feed_away, d) for d in near}

    own_meta.wait()
    own_tok.wait()
    own_table.wait()
    tok_ring.wait()
    for copy in (*meta_copies, *table_copies):
        copy.wait_recv()
    for hop in first_hops.values():
        hop[1].wait_recv()
    for copy in first_last:
        copy.wait_recv()
    odd = lax.rem(at.x, 2) == 1

    def project(s, carry):
        values = tok[s].astype(F32)
        scale = lax.rsqrt(jnp.mean(values * values, axis=-1, keepdims=True) + epsilon)
        total = jnp.zeros((128, 768), F32)
        for f in range(16):
            span = pl.ds(f * 128, 128)
            normed[s, :, span] = (tok[s, :, span].astype(F32) * scale * meta[f, 8:9, :]).astype(BF)
        for g in range(8):
            total += dot(
                normed[s, :, pl.ds(g * 256, 256)],
                w_first[g // 2, g % 2].reshape(256, 768),
            )
        cosine, sine = wheel(table[s])
        for t in range(4):
            span = slice(t * 128, t * 128 + 128)
            queries[s, :, span] = (turn(total[:, span], cosine, sine) * 0.125).astype(BF)
        key, value = total[:, 512:640], total[:, 640:768]
        key = turn(jnp.where(odd, pltpu.roll(key, 64, 1), key), cosine, sine)
        value = jnp.where(odd, value, pltpu.roll(value, 64, 1))
        keys[s, at.ctx] = jnp.where(lanes((128, 128)) < 64, key, value).astype(BF)
        return carry

    lax.fori_loop(0, 4, project, 0)
    mine = keys.at[:, at.ctx]
    over = net.send(mine, mine, at.z_hi())
    key_copies = [net.send(mine, mine, at.to_y(d)) for d in near]
    down_z = [
        net.send(down_in.at[pl.ds(0, 176)], w_down.at[at.z, at.c, pl.ds(0, 176)], at.z_in()),
        net.send(down_in.at[pl.ds(176, 176)], w_down.at[at.z, at.c, pl.ds(176, 176)], at.z_out()),
    ]
    down_c = [net.send(down_in, w_down.at[at.z, at.c], at.core())]
    dy_ring.forward()
    over.wait_recv()
    theirs = keys.at[:, (1 - at.hi) * 4 + at.y]
    key_copies += [net.send(theirs, theirs, at.to_y(d)) for d in near]
    for d in near:
        for copy in feed_shared[d]:
            copy.wait_recv()
        feed_hops[d] = relay(w_feed, d)
    own_out.wait()
    for copy in out_z:
        copy.wait_recv()
    out_c.append(net.send(w_out.at[1 - at.z, at.c], w_out.at[1 - at.z, at.c], at.core()))
    for copy in out_c:
        copy.wait_recv()
    for copy in key_copies:
        copy.wait_recv()

    def attend(s):
        masks = key_masks(meta, at.xs(owner[s]) * 4 + at.zc, at.ctx)
        for j in range(8):
            mask[:, j * 128 : j * 128 + 128] = masks[j]
        both = keys[s].reshape(1024, 128).astype(F32)
        lane = lanes(both.shape)
        key = jnp.where(lane < 64, both, 0.0)
        value = jnp.where(lane < 64, 0.0, both)
        key_pair = (key.astype(BF), pltpu.roll(key, 64, 1).astype(BF))
        value_pair = (pltpu.roll(value, 64, 1).astype(BF), value.astype(BF))
        head_lane = lanes((128, 128))
        log_rows = jnp.zeros((128, 128), F32)
        for t in range(4):
            query = queries[s, :, t * 128 : t * 128 + 128]
            total = jnp.zeros((128, 128), F32)
            for p in range(2):
                scores = dot_t(query, key_pair[p]) + mask[...]
                largest = jnp.max(scores, axis=-1, keepdims=True)
                weights = jnp.exp(scores - largest)
                amount = jnp.sum(weights, axis=-1, keepdims=True)
                total += dot(weights.astype(BF), value_pair[p]) * (1.0 / amount)
                log_rows = jnp.where(
                    head_lane == 2 * t + p, largest + jnp.log(amount), log_rows
                )
            mixed[s, :, t * 128 : t * 128 + 128] = total.astype(BF)
        logs[s] = log_rows
        return dot(mixed[s], w_out[...].reshape(512, 2048))

    sum_copies = []
    for s, d in ((3, 2), (1, 3), (2, 1)):
        sums[s - 1] = attend(s).astype(BF)
        sum_copies.append(net.send(sums.at[s - 1], got.at[s - 1], at.to_x(d)))
    own = attend(0)
    feed_last = []
    for d in (0, *near):
        feed_hops[d][0].wait_recv()
        feed_last.append(relay_core(w_feed, d))
    for copy in sum_copies:
        copy.wait_recv()
    total = tok[0].astype(F32) + own
    for i in range(3):
        total += got[i].astype(F32)
    residual[...] = total
    scale = lax.rsqrt(jnp.mean(total * total, axis=-1, keepdims=True) + epsilon)
    for f in range(16):
        span = pl.ds(f * 128, 128)
        normed_two[0, :, span] = (residual[:, span] * scale * meta[f, 9:10, :]).astype(BF)
    two_ring = Ring(at, net, normed_two.at[0], normed_two)
    for copy in down_z:
        copy.wait_recv()
    down_c.append(net.send(w_down.at[1 - at.z, at.c], w_down.at[1 - at.z, at.c], at.core()))
    two_ring.forward()
    for copy in store:
        copy.wait()
    for hop in feed_hops.values():
        hop[1].wait_recv()
    for copy in (*down_c, *feed_last):
        copy.wait_recv()
    dy_ring.wait()
    two_ring.wait()
    net.finish()


def forward(meta, table, tok, q, k, v, o, gate, up, down, dy):
    shape = jax.ShapeDtypeStruct
    outs = (
        shape((16, 16, 128), F32),
        shape((4, 64, 128), F32),
        shape((4, 128, 2048), BF),
        shape((4, 128, 2048), BF),
        shape((4, 128, 512), BF),
        shape((4, 8, 128, 128), BF),
        shape((4, 128, 128), F32),
        shape((4, 128, 512), BF),
        shape((128, 2048), F32),
        shape((4, 128, 2048), BF),
        shape((4, 2, 2, 128, 768), BF),
        shape((2, 2, 128, 2048), BF),
        shape((4, 2, 2, 128, 2816), BF),
        shape((2, 2, 352, 2048), BF),
        shape((4, 128, 2048), BF),
    )
    return pl.pallas_call(
        forward_kernel,
        name="forward",
        out_shape=outs,
        in_specs=[EVERYWHERE] * 11,
        out_specs=(ON_CHIP,) * 12 + (EVERYWHERE,) * 3,
        scratch_shapes=[
            pltpu.VMEM((3, 128, 2048), BF),
            pltpu.VMEM((3, 128, 2048), BF),
            pltpu.VMEM((128, 1024), F32),
            pltpu.VMEM((128, 2816), BF),
            pltpu.VMEM((352, 2048), BF),
            pltpu.VMEM((128, 2048), BF),
            pltpu.SemaphoreType.DMA((112,)),
            pltpu.SemaphoreType.DMA((112,)),
            pltpu.SemaphoreType.DMA((20,)),
        ],
        compiler_params=pltpu.CompilerParams(
            collective_id=1, has_side_effects=True, vmem_limit_bytes=VMEM_LIMIT
        ),
    )(meta, table, tok, q, k, v, o, gate, up, down, dy)


NEAR = (1, 3, 2)
CHUNKS = ((0, 512), (512, 512), (1024, 384))


def feed_kernel(
    n2,
    dy,
    residual,
    meta,
    feed_in,
    down_in,
    part_y,
    dr,
    dz,
    keep_feed,
    keep_down,
    gain_term,
    w_feed,
    w_down,
    hid,
    dgu,
    part_two,
    got_two,
    core_feed,
    core_down,
    gain,
    send_sems,
    recv_sems,
    local_sems,
):
    at = Spot()
    net = Copies(send_sems, recv_sems, local_sems)
    loads = []
    for start, size in CHUNKS:
        spans = pl.ds(start, size), pl.ds(1408 + start, size)
        loads.append(
            [net.local(feed_in.at[..., t], w_feed.at[..., t]) for t in spans]
            + [net.local(down_in.at[spans[0]], w_down.at[spans[0]])]
        )
    greet([at.to_x(d) for d in NEAR] + [at.z_in(), at.z_out(), at.core()])
    for f in range(16):
        gain[:, f * 128 : f * 128 + 128] = meta[f, 9:10, :]

    two_copies = []
    for first in (2, 0):
        rows = slice(first * 128, first * 128 + 256)
        tokens_here = n2[first : first + 2].reshape(256, 2048)
        cotangent_here = dy[first : first + 2].reshape(256, 2048)
        for (start, size), load in zip(CHUNKS, loads):
            if first:
                for copy in load:
                    copy.wait()
            gate = jnp.zeros((256, size), F32)
            up = jnp.zeros((256, size), F32)
            for x in range(4):
                some = tokens_here[:, x * 512 : x * 512 + 512]
                gate += dot(some, w_feed[x, :, :, :, start : start + size].reshape(512, size))
                up += dot(
                    some,
                    w_feed[x, :, :, :, 1408 + start : 1408 + start + size].reshape(512, size),
                )
            dhid = dot_t(cotangent_here, w_down[start : start + size, :])
            sigmoid = 1.0 / (1.0 + jnp.exp(-gate))
            activated = gate * sigmoid
            hid[rows, start : start + size] = (activated * up).astype(BF)
            slope = sigmoid * (1.0 + gate * (1.0 - sigmoid))
            dgu[rows, start : start + size] = (dhid * up * slope).astype(BF)
            dgu[rows, 1408 + start : 1408 + start + size] = (dhid * activated).astype(BF)
        for x in range(4):
            span = slice(x * 512, x * 512 + 512)
            term = dot_t(dgu[rows, :], w_feed[x].reshape(512, 2816))
            part_two[first + 1, :, span] = term[128:].astype(BF)
            if first == 0:
                dr[:, span] = term[:128]
            else:
                part_two[first, :, span] = term[:128].astype(BF)
        for s, d in ((3, 2), (2, 1)) if first else ((1, 3),):
            two_copies.append(net.send(part_two.at[s], got_two.at[s - 1], at.to_x(d)))

    core_copies, z_copies = [], []

    def pass_z(x):
        core_copies[x].wait_recv()
        w_feed[x, 1 - at.z, at.c] = (
            w_feed[x, 1 - at.z, at.c].astype(F32) + core_feed[x, 1 - at.z].astype(F32)
        ).astype(BF)
        z_copies.append(
            net.send(
                w_feed.at[x, 1 - at.z, at.c],
                keep_feed.at[x],
                at.z_out() if x % 2 else at.z_in(),
            )
        )

    for x in range(4):
        some = n2[:, :, x * 512 : x * 512 + 512].reshape(512, 512)
        for start, size in ((0, 1408), (1408, 1408)):
            w_feed[x, :, :, :, start : start + size] = (
                t_dot(some, dgu[:, start : start + size])
                .astype(BF)
                .reshape(2, 2, 128, size)
            )
        core_copies.append(net.send(w_feed.at[x, :, 1 - at.c], core_feed.at[x], at.core()))
        if x:
            pass_z(x - 1)
    for first in (2, 0):
        rows = slice(first * 128, first * 128 + 256)
        for j in range(4):
            span = slice(j * 512, j * 512 + 512)
            term = dot(hid[rows, :], w_down[:, span]).astype(BF)
            part_y[first, :, span] = term[:128]
            part_y[first + 1, :, span] = term[128:]
        if first:
            pass_z(3)

    for copy in two_copies:
        copy.wait_recv()
    grad = dr[...]
    for i in range(3):
        grad += got_two[i].astype(F32)
    values = residual[...]
    scale = lax.rsqrt(jnp.mean(values * values, axis=-1, keepdims=True) + epsilon)
    gain_term[...] = jnp.sum(grad * values * scale, axis=0, keepdims=True)
    weighted = grad * gain[...]
    inner = jnp.mean(weighted * values, axis=-1, keepdims=True)
    dr[...] = dy[0].astype(F32) + weighted * scale - values * (scale * scale * scale * inner)
    dz[0] = dr[...].astype(BF)
    ring = Ring(at, net, dz.at[0], dz)

    for start, size in CHUNKS:
        w_down[start : start + size, :] = t_dot(
            hid[:, start : start + size], dy[...].reshape(512, 2048)
        ).astype(BF)

    def down_rows(z, c):
        return pl.ds(pl.multiple_of((z * 2 + c) * 352, 16), 352)

    down_copies = [
        net.send(w_down.at[down_rows(z, 1 - at.c)], core_down.at[z], at.core()) for z in range(2)
    ]
    ring.forward()
    for z in range(2):
        down_copies[z].wait_recv()
    for i, z in enumerate((at.z, 1 - at.z)):
        keep_down[i] = (
            w_down[down_rows(z, at.c), :].astype(F32) + core_down[z].astype(F32)
        ).astype(BF)
    for x in range(4):
        z_copies[x].wait_recv()
        keep_feed[x] = (
            keep_feed[x].astype(F32)
            + w_feed[x, at.z, at.c].astype(F32)
            + core_feed[x, at.z].astype(F32)
        ).astype(BF)
    ring.wait()
    net.finish()


def feed(n2, dy, residual, meta, w_feed, w_down):
    shape = jax.ShapeDtypeStruct
    return pl.pallas_call(
        feed_kernel,
        name="feed",
        out_shape=(
            shape((4, 128, 2048), BF),
            shape((128, 2048), F32),
            shape((4, 128, 2048), BF),
            shape((4, 128, 2816), BF),
            shape((2, 352, 2048), BF),
            shape((1, 2048), F32),
        ),
        in_specs=[ON_CHIP] * 4 + [EVERYWHERE] * 2,
        out_specs=(ON_CHIP,) * 6,
        scratch_shapes=[
            pltpu.VMEM((4, 2, 2, 128, 2816), BF),
            pltpu.VMEM((1408, 2048), BF),
            pltpu.VMEM((512, 1408), BF),
            pltpu.VMEM((512, 2816), BF),
            pltpu.VMEM((4, 128, 2048), BF),
            pltpu.VMEM((3, 128, 2048), BF),
            pltpu.VMEM((4, 2, 128, 2816), BF),
            pltpu.VMEM((2, 352, 2048), BF),
            pltpu.VMEM((1, 2048), F32),
            pltpu.SemaphoreType.DMA((32,)),
            pltpu.SemaphoreType.DMA((32,)),
            pltpu.SemaphoreType.DMA((12,)),
        ],
        compiler_params=pltpu.CompilerParams(
            collective_id=2, has_side_effects=True, vmem_limit_bytes=VMEM_LIMIT
        ),
    )(n2, dy, residual, meta, w_feed, w_down)


class Sums:
    def __init__(self, at, net):
        self.at, self.net = at, net

    def over_y(self, halves, own, relay, joined, got, out):
        at, net = self.at, self.net
        up, down, far = halves(at.ys(1)), halves(at.ys(3)), halves(at.ys(2))
        passed = [
            net.send(far[0], relay[0], at.to_y(1)),
            net.send(far[1], relay[1], at.to_y(3)),
        ]
        copies = [
            net.send(up[1], got[0][1], at.to_y(1)),
            net.send(down[0], got[1][0], at.to_y(3)),
        ]
        yield
        for i, (source, target, peer) in enumerate(
            ((up[0], got[0][0], at.to_y(1)), (down[1], got[1][1], at.to_y(3)))
        ):
            passed[i].wait_recv()
            joined[i][...] = (source[...].astype(F32) + relay[i][...].astype(F32)).astype(BF)
            copies.append(net.send(joined[i], target, peer))
        yield
        for copy in copies:
            copy.wait_recv()
        for h in range(2):
            out[h][...] = (
                own[h][...].astype(F32) + got[0][h][...].astype(F32) + got[1][h][...].astype(F32)
            ).astype(BF)

    def around_y(self, halves):
        at, net = self.at, self.net
        copies = [net.send(h, h, at.to_y(d)) for d in (1, 3) for h in halves(at.y)]
        yield
        copies[0].wait_recv()
        far = halves(at.ys(3))[0]
        last = [net.send(far, far, at.to_y(1))]
        copies[3].wait_recv()
        far = halves(at.ys(1))[1]
        last.append(net.send(far, far, at.to_y(3)))
        yield
        for copy in (copies[1], copies[2], *last):
            copy.wait_recv()

    def over_z_hi(self, mine, got):
        copy = self.net.send(mine, got, self.at.z_hi())
        yield
        copy.wait_recv()
        got[...] = (got[...].astype(F32) + mine[...].astype(F32)).astype(BF)

    def columns(self, terms, span, relay, joined, got_y, mine, got_z, place, halves):
        at, net = self.at, self.net

        def parts(y):
            rows = pl.ds(pl.multiple_of(y * 32, 32), 32)
            return [terms.at[h : h + 2, rows, span] for h in (0, 2)]

        pair = lambda ref: [ref.at[h : h + 2, :, span] for h in (0, 2)]
        ends = lambda ref: [ref.at[i, :, :, span] for i in range(2)]
        yield from self.over_y(
            parts,
            parts(at.y),
            ends(relay),
            ends(joined),
            [pair(got_y.at[i]) for i in range(2)],
            pair(mine),
        )
        yield from self.over_z_hi(mine.at[:, :, span], got_z.at[:, :, span])
        here = net.local(got_z.at[at.x, :, span], place(at.x))
        copies = [
            net.send(got_z.at[at.xs(d), :, span], place(at.x), at.to_x(d)) for d in NEAR
        ]
        here.wait()
        yield
        for copy in copies:
            copy.wait_recv()
        yield from self.around_y(halves)

    def rows(self, terms, relay, joined, got_y, mine, got_z, out):
        at, net = self.at, self.net
        half = terms.shape[0] // 2
        starts = (0, half)

        def split(ref, y):
            columns = pl.ds(pl.multiple_of(y * 512, 128), 512)
            return [ref.at[pl.ds(h, half), columns] for h in starts]

        pair = lambda ref: [ref.at[pl.ds(h, half)] for h in starts]
        yield from self.over_y(
            lambda y: split(terms, y),
            split(terms, at.y),
            [relay.at[i] for i in range(2)],
            [joined.at[i] for i in range(2)],
            [pair(got_y.at[i]) for i in range(2)],
            pair(mine),
        )
        yield from self.over_z_hi(mine, got_z)
        here = [
            net.local(got_z.at[pl.ds(h, half)], place)
            for h, place in zip(starts, split(out, at.y))
        ]
        for copy in here:
            copy.wait()
        yield from self.around_y(lambda y: split(out, y))

    def down(self, terms, got_z):
        at, net = self.at, self.net
        copies = [
            net.send(terms.at[1, pl.ds(r, 176)], got_z.at[pl.ds(r, 176)], peer)
            for r, peer in ((0, at.z_in()), (176, at.z_out()))
        ]
        yield
        for copy in copies:
            copy.wait_recv()
        got_z[...] = (got_z[...].astype(F32) + terms[0].astype(F32)).astype(BF)

    def first(self, terms, span, got_core, got_z):
        at, net = self.at, self.net
        copy = net.send(
            terms.at[:, :, 1 - at.c, :, span], got_core.at[:, :, :, span], at.core()
        )
        yield
        copy.wait_recv()
        for r in range(4):
            terms[r, 1 - at.z, at.c, :, span] = (
                terms[r, 1 - at.z, at.c, :, span].astype(F32)
                + got_core[r, 1 - at.z, :, span].astype(F32)
            ).astype(BF)
        copies = [
            net.send(
                terms.at[r : r + 2, 1 - at.z, at.c, :, span], got_z.at[r : r + 2, :, span], peer
            )
            for r, peer in ((0, at.z_in()), (2, at.z_out()))
        ]
        yield
        for copy in copies:
            copy.wait_recv()
        for r in range(4):
            got_z[r, :, span] = (
                got_z[r, :, span].astype(F32)
                + terms[r, at.z, at.c, :, span].astype(F32)
                + got_core[r, at.z, :, span].astype(F32)
            ).astype(BF)

    def out(self, terms, got_core, got_z):
        at, net = self.at, self.net
        copy = net.send(terms.at[:, 1 - at.c], got_core, at.core())
        yield
        copy.wait_recv()
        terms[1 - at.z, at.c] = (
            terms[1 - at.z, at.c].astype(F32) + got_core[1 - at.z].astype(F32)
        ).astype(BF)
        copies = [
            net.send(
                terms.at[1 - at.z, at.c, pl.ds(r, 64)], got_z.at[pl.ds(r, 64)], peer
            )
            for r, peer in ((0, at.z_in()), (64, at.z_out()))
        ]
        yield
        for copy in copies:
            copy.wait_recv()
        got_z[...] = (
            got_z[...].astype(F32)
            + terms[at.z, at.c].astype(F32)
            + got_core[at.z].astype(F32)
        ).astype(BF)


def chained(*parts):
    for part in parts:
        yield from part


def backward_kernel(
    dz,
    dr,
    tok,
    meta,
    table,
    queries,
    keys,
    logs,
    mixed,
    normed_in,
    first_in,
    w_out,
    feed_terms,
    down_terms,
    gain_two,
    part_y,
    residual,
    dx,
    output,
    gains,
    gate_sum,
    up_sum,
    down_sum,
    out_sum,
    first_sum,
    normed,
    w_first,
    got_out,
    dmix,
    mask,
    probs,
    scores_grad,
    pre,
    key_part,
    key_got,
    part,
    got_part,
    out_terms,
    out_core,
    out_z,
    first_terms,
    first_core,
    first_z,
    feed_r,
    feed_j,
    feed_y,
    feed_mine,
    feed_z,
    down_zz,
    down_r,
    down_j,
    down_y,
    down_mine,
    down_z,
    out_r,
    out_j,
    out_y,
    out_mine,
    out_zz,
    first_r,
    first_j,
    first_y,
    first_mine,
    first_zz,
    gain,
    gain_send,
    gain_got,
    gain_part,
    gain_last,
    send_sems,
    recv_sems,
    local_sems,
):
    at = Spot()
    net = Copies(send_sems, recv_sems, local_sems)
    slot = {1: 1, 3: 2, 2: 3}
    owner = {0: 0, 1: 3, 2: 1, 3: 2}

    def to_ctx(k):
        return (lax.rem(at.ctx + k, 8), at.f)

    load_normed = net.local(normed_in, normed)
    load_first = net.local(first_in, w_first)
    greet(
        [at.fsdp(d) for d in range(1, 16)] + [to_ctx(k) for k in range(1, 8)] + [at.z_out()]
    )
    sums = Sums(at, net)

    def rows_of(y):
        return pl.ds(pl.multiple_of(y * 32, 32), 32)

    def feed_chain(span, out):
        return sums.columns(
            feed_terms,
            span,
            feed_r,
            feed_j,
            feed_y,
            feed_mine,
            feed_z,
            lambda r: out.at[rows_of(at.y), pl.ds(pl.multiple_of(r * 1408, 128), 1408)],
            lambda y: [out.at[rows_of(y), pl.ds(h, 2816)] for h in (0, 2816)],
        )

    gate_chain = feed_chain(slice(0, 1408), gate_sum)
    up_chain = feed_chain(slice(1408, 2816), up_sum)
    down_chain = chained(
        sums.down(down_terms, down_zz),
        sums.rows(down_zz, down_r, down_j, down_y, down_mine, down_z, down_sum),
    )
    out_chain = chained(
        sums.out(out_terms, out_core, out_z),
        sums.rows(out_z, out_r, out_j, out_y, out_mine, out_zz, out_sum),
    )

    def first_chain(span):
        return chained(
            sums.first(first_terms, span, first_core, first_z),
            sums.columns(
                first_z,
                span,
                first_r,
                first_j,
                first_y,
                first_mine,
                first_zz,
                lambda r: first_sum.at[r, rows_of(at.y), span],
                lambda y: [first_sum.at[h : h + 2, rows_of(y), span] for h in (0, 2)],
            ),
        )

    query_chain = first_chain(slice(0, 512))
    key_chain = first_chain(slice(512, 640))

    def step(*chains):
        for chain in chains:
            next(chain, None)

    step(gate_chain, down_chain)
    y_copies = [
        net.send(part_y.at[s], got_out.at[s - 1], at.to_x(d)) for s, d in ((3, 2), (1, 3), (2, 1))
    ]
    for f in range(16):
        gain[:, f * 128 : f * 128 + 128] = meta[f, 8:9, :]
    weight = w_out[...].reshape(512, 2048)
    for s in range(4):
        dmix[s] = dot_t(dz[s], weight).astype(BF)
    for j in range(2):
        span = slice(j * 1024, j * 1024 + 1024)
        out_terms[:, :, :, span] = (
            t_dot(mixed[...].reshape(512, 512), dz[:, :, span].reshape(512, 1024))
            .astype(BF)
            .reshape(2, 2, 128, 1024)
        )
    step(out_chain)

    def attend(s):
        masks = key_masks(meta, at.xs(owner[s]) * 4 + at.zc, at.ctx)
        for j in range(8):
            mask[:, j * 128 : j * 128 + 128] = masks[j]
        both = keys[s].reshape(1024, 128).astype(F32)
        lane = lanes(both.shape)
        key = jnp.where(lane < 64, both, 0.0)
        value = jnp.where(lane < 64, 0.0, both)
        key_pair = (key.astype(BF), pltpu.roll(key, 64, 1).astype(BF))
        value_pair = (pltpu.roll(value, 64, 1).astype(BF), value.astype(BF))
        cosine, sine = wheel(table[s])
        for t in range(4):
            span = slice(t * 128, t * 128 + 128)
            query, grad = queries[s, :, span], dmix[s, :, span]
            total = jnp.zeros((128, 128), F32)
            for p in range(2):
                scores = dot_t(query, key_pair[p]) + mask[...]
                prob = jnp.exp(scores - logs[s, :, 2 * t + p : 2 * t + p + 1])
                prob_grad = dot_t(grad, value_pair[p])
                inner = jnp.sum(prob * prob_grad, axis=-1, keepdims=True)
                low = (prob * (prob_grad - inner)).astype(BF)
                probs[p, span, :] = prob.astype(BF)
                scores_grad[p, span, :] = low
                total += dot(low, key_pair[p])
            pre[s, :, span] = turn(total * 0.125, cosine, -sine).astype(BF)
        stack = lambda a: jnp.concatenate([a[s, :, t * 128 : t * 128 + 128] for t in range(4)], axis=0)
        query, grad = stack(queries), stack(dmix)
        half = lanes((1024, 128)) < 64
        key_grad = t_dot(scores_grad[0], query), t_dot(scores_grad[1], query)
        value_grad = t_dot(probs[0], grad), t_dot(probs[1], grad)
        total = jnp.where(
            half,
            key_grad[0] + pltpu.roll(key_grad[1], 64, 1),
            pltpu.roll(value_grad[0], 64, 1) + value_grad[1],
        )
        for j in range(8):
            key_part[j, s] = total[j * 128 : j * 128 + 128].astype(BF)

    def send_keys(first):
        return [
            net.send(
                key_part.at[lax.rem(at.ctx + k, 8), first : first + 2],
                key_got.at[k - 1, first : first + 2],
                to_ctx(k),
            )
            for k in range(1, 8)
        ]

    attend(0)
    step(out_chain, gate_chain)
    attend(1)
    key_copies = send_keys(0)
    step(up_chain)
    attend(2)
    step(out_chain)
    attend(3)
    key_copies += send_keys(2)
    step(gate_chain, down_chain, up_chain)
    load_normed.wait()
    for x in range(4):
        first_terms[x, :, :, :, 0:512] = (
            t_dot(
                normed[:, :, x * 512 : x * 512 + 512].reshape(512, 512),
                pre[:, :, 0:512].reshape(512, 512),
            )
            .astype(BF)
            .reshape(2, 2, 128, 512)
        )
    step(query_chain, gate_chain, query_chain, out_chain, down_chain)
    for copy in key_copies:
        copy.wait_recv()
    odd = lax.rem(at.x, 2) == 1
    half = lanes((128, 128)) < 64
    windows = []
    for s in range(4):
        total = key_part[at.ctx, s].astype(F32)
        for k in range(7):
            total += key_got[k, s].astype(F32)
        cosine, sine = wheel(table[s])
        total = jnp.where(half, turn(total, cosine, -sine), total)
        pre[s, :, 512:640] = total.astype(BF)
        moved = pltpu.roll(total, 64, 1)
        windows.append(
            jnp.concatenate(
                [
                    jnp.where(half, jnp.where(odd, 0.0, total), jnp.where(odd, moved, 0.0)),
                    jnp.where(half, jnp.where(odd, 0.0, moved), jnp.where(odd, total, 0.0)),
                ],
                axis=1,
            ).astype(BF)
        )
    window = jnp.concatenate(windows, axis=0)
    load_first.wait()
    for x in range(4):
        span = slice(x * 512, x * 512 + 512)
        term = dot_t(
            pre[:, :, 0:512].reshape(512, 512), w_first[x, :, :, :, 0:512].reshape(512, 512)
        ) + dot_t(window, w_first[x, :, :, :, 512:768].reshape(512, 256))
        dx[:, span] = term[:128]
        for s in range(1, 4):
            part[s, :, span] = term[s * 128 : s * 128 + 128].astype(BF)
    part_copies = [
        net.send(part.at[s], got_part.at[s - 1], at.to_x(d)) for s, d in ((3, 2), (1, 3), (2, 1))
    ]
    for x in range(4):
        first_terms[x, :, :, :, 512:640] = (
            t_dot(
                normed[:, :, x * 512 : x * 512 + 512].reshape(512, 512),
                pre[:, :, 512:640].reshape(512, 128),
            )
            .astype(BF)
            .reshape(2, 2, 128, 128)
        )
    step(key_chain, query_chain, key_chain, gate_chain, up_chain, down_chain, out_chain)
    for copy in y_copies:
        copy.wait_recv()
    total = residual[...] + part_y[0].astype(F32)
    for i in range(3):
        total += got_out[i].astype(F32)
    output[...] = total.astype(BF)
    step(key_chain, query_chain, up_chain, gate_chain)
    for copy in part_copies:
        copy.wait_recv()
    grad = dx[...]
    for i in range(3):
        grad += got_part[i].astype(F32)
    values = tok[...].astype(F32)
    scale = lax.rsqrt(jnp.mean(values * values, axis=-1, keepdims=True) + epsilon)
    gain_one = jnp.sum(grad * values * scale, axis=0, keepdims=True)
    weighted = grad * gain[...]
    inner = jnp.mean(weighted * values, axis=-1, keepdims=True)
    dx[...] = dr[...] + weighted * scale - values * (scale * scale * scale * inner)
    for f in range(16):
        span = slice(f * 128, f * 128 + 128)
        gain_send[f] = jnp.concatenate(
            [gain_one[:, span], gain_two[:, span], jnp.zeros((6, 128), F32)], axis=0
        )
    gain_copies = [
        net.send(gain_send.at[lax.rem(at.f + d, 16)], gain_got.at[d - 1], at.fsdp(d))
        for d in range(1, 16)
    ]
    everyone = (key_chain, query_chain, gate_chain, up_chain, down_chain, out_chain)
    step(*everyone)
    for copy in gain_copies:
        copy.wait_recv()
    total = gain_send[at.f]
    for d in range(15):
        total += gain_got[d]
    gain_part[...] = total
    last_copies = [net.send(gain_part, gain_last.at[k - 1], to_ctx(k)) for k in range(1, 8)]
    for _ in range(4):
        step(*everyone)
    for copy in last_copies:
        copy.wait_recv()
    total = gain_part[...]
    for k in range(7):
        total += gain_last[k]
    gains[...] = total
    for _ in range(8):
        step(*everyone)
    net.finish()


def backward(*operands):
    shape = jax.ShapeDtypeStruct
    vmem = lambda *dims: pltpu.VMEM(dims, BF)
    wide = lambda *dims: pltpu.VMEM(dims, F32)
    return pl.pallas_call(
        backward_kernel,
        name="backward",
        out_shape=(
            shape((128, 2048), F32),
            shape((128, 2048), BF),
            shape((8, 128), F32),
            shape((128, 5632), BF),
            shape((128, 5632), BF),
            shape((352, 2048), BF),
            shape((128, 2048), BF),
            shape((4, 128, 640), BF),
        ),
        in_specs=[ON_CHIP] * 9 + [EVERYWHERE] * 2 + [ON_CHIP] * 6,
        out_specs=(ON_CHIP,) * 8,
        scratch_shapes=[
            vmem(4, 128, 2048),
            vmem(4, 2, 2, 128, 768),
            vmem(3, 128, 2048),
            vmem(4, 128, 512),
            wide(128, 1024),
            vmem(2, 512, 1024),
            vmem(2, 512, 1024),
            vmem(4, 128, 640),
            vmem(8, 4, 128, 128),
            vmem(7, 4, 128, 128),
            vmem(4, 128, 2048),
            vmem(3, 128, 2048),
            vmem(2, 2, 128, 2048),
            vmem(2, 128, 2048),
            vmem(128, 2048),
            vmem(4, 2, 2, 128, 640),
            vmem(4, 2, 128, 640),
            vmem(4, 128, 640),
            vmem(2, 2, 32, 2816),
            vmem(2, 2, 32, 2816),
            vmem(2, 4, 32, 2816),
            vmem(4, 32, 2816),
            vmem(4, 32, 2816),
            vmem(352, 2048),
            vmem(2, 176, 512),
            vmem(2, 176, 512),
            vmem(2, 352, 512),
            vmem(352, 512),
            vmem(352, 512),
            vmem(2, 64, 512),
            vmem(2, 64, 512),
            vmem(2, 128, 512),
            vmem(128, 512),
            vmem(128, 512),
            vmem(2, 2, 32, 640),
            vmem(2, 2, 32, 640),
            vmem(2, 4, 32, 640),
            vmem(4, 32, 640),
            vmem(4, 32, 640),
            wide(1, 2048),
            wide(16, 8, 128),
            wide(15, 8, 128),
            wide(8, 128),
            wide(7, 8, 128),
            pltpu.SemaphoreType.DMA((160,)),
            pltpu.SemaphoreType.DMA((160,)),
            pltpu.SemaphoreType.DMA((16,)),
        ],
        compiler_params=pltpu.CompilerParams(
            collective_id=3, has_side_effects=True, vmem_limit_bytes=VMEM_LIMIT
        ),
    )(*operands)


def per_device(
    tokens,
    positions,
    attention_gain,
    query_weight,
    key_weight,
    value_weight,
    out_weight,
    feed_gain,
    gate_weight,
    up_weight,
    down_weight,
    cotangent,
):
    width = tokens.shape[3]
    places = positions.reshape(2, 8, 64).transpose(1, 0, 2).reshape(8, 128).astype(F32)
    meta = jnp.concatenate(
        [places, attention_gain[None], feed_gain[None], jnp.zeros((6, 128), F32)], axis=0
    )
    own_places = lax.dynamic_index_in_dim(places, lax.axis_index("ctx"), 0, keepdims=False)[:, None]
    angles = own_places * frequencies(HEAD_DIM)[None]
    table = jnp.concatenate(
        [jnp.cos(angles[:64]), jnp.sin(angles[:64]), jnp.cos(angles[64:]), jnp.sin(angles[64:])],
        axis=1,
    )
    token_rows = tokens.reshape(128, width)
    branch_grad = cotangent.reshape(128, width)
    (
        meta,
        table,
        _,
        normed,
        query_rot,
        keys,
        logs,
        mixed_low,
        residual,
        normed_two,
        w_first,
        w_out,
        w_feed,
        w_down,
        branch4,
    ) = forward(
        meta,
        table,
        token_rows,
        query_weight,
        key_weight,
        value_weight,
        out_weight,
        gate_weight,
        up_weight,
        down_weight,
        branch_grad,
    )
    part_y, residual_grad, branch_low, feed_terms, down_terms, gain_two_term = feed(
        normed_two, branch4, residual, meta, w_feed, w_down.reshape(1408, width)
    )
    input_grad, output, gains, gate_sum, up_sum, down_sum, out_sum, first_sum = backward(
        branch_low,
        residual_grad,
        token_rows,
        meta,
        table,
        query_rot,
        keys,
        logs,
        mixed_low,
        normed,
        w_first,
        w_out,
        feed_terms,
        down_terms,
        gain_two_term,
        part_y,
        residual,
    )
    first_sum = first_sum.transpose(1, 0, 2).astype(F32)
    return (
        output.reshape(tokens.shape),
        input_grad.reshape(tokens.shape),
        gains[0],
        first_sum[:, :, :512].reshape(128, -1),
        first_sum[:, :, 512:576].reshape(128, -1),
        first_sum[:, :, 576:].reshape(128, -1),
        out_sum.astype(F32),
        gains[1],
        gate_sum.astype(F32),
        up_sum.astype(F32),
        down_sum.astype(F32),
    )


def solution(mesh):
    rows = P("fsdp", None)
    blocks = P("fsdp", None, "ctx", None)
    return jax.shard_map(
        per_device,
        mesh=mesh,
        in_specs=(
            blocks,
            P("fsdp", None, None),
            P("fsdp"),
            rows,
            rows,
            rows,
            rows,
            P("fsdp"),
            rows,
            rows,
            rows,
            blocks,
        ),
        out_specs=(blocks, blocks, P("fsdp"), rows, rows, rows, rows, P("fsdp"), rows, rows, rows),
        check_vma=False,
    )
```

```python
import jax
import jax.numpy as jnp
from jax import lax
from jax.experimental import pallas as pl
from jax.experimental.pallas import tpu as pltpu
from jax.sharding import PartitionSpec as P

HEAD_DIM = 64
BF = jnp.bfloat16
F32 = jnp.float32
epsilon = 1e-05


def dot(a, b):
    return jnp.dot(a, b, preferred_element_type=F32)


def dot_t(a, b):
    return lax.dot_general(a, b, (((1,), (1,)), ((), ())), preferred_element_type=F32)


def t_dot(a, b):
    return lax.dot_general(a, b, (((0,), (0,)), ((), ())), preferred_element_type=F32)


def frequencies(head_width):
    return 10000.0 ** (-(2.0 * jnp.arange(head_width // 2, dtype=F32)) / head_width)


MESH = pl.DeviceIdType.MESH
EVERYWHERE = pl.BlockSpec(memory_space=pl.ANY)
ON_CHIP = pl.BlockSpec(memory_space=pltpu.VMEM)
VMEM_LIMIT = 62 * 2**20


class Spot:
    def __init__(self):
        ctx, f = lax.axis_index("ctx"), lax.axis_index("fsdp")
        self.ctx, self.f = ctx, f
        self.y, self.hi = lax.rem(ctx, 4), ctx // 4
        self.x, self.z, self.c = f // 4, lax.rem(f // 2, 2), lax.rem(f, 2)
        self.zc = lax.rem(f, 4)

    def xs(self, d):
        return lax.rem(self.x + d, 4)

    def ys(self, d):
        return lax.rem(self.y + d, 4)

    def to_x(self, d):
        return (self.ctx, self.xs(d) * 4 + self.zc)

    def to_y(self, d):
        return (self.hi * 4 + self.ys(d), self.f)

    def z_in(self):
        return (self.ctx, self.x * 4 + (1 - self.z) * 2 + self.c)

    def z_out(self):
        return ((1 - self.hi) * 4 + self.y, self.x * 4 + (1 - self.z) * 2 + self.c)

    def z_hi(self):
        return ((1 - self.hi) * 4 + self.y, self.f)

    def core(self):
        return (self.ctx, self.x * 4 + self.z * 2 + 1 - self.c)

    def fsdp(self, d):
        return (self.ctx, lax.rem(self.f + d, 16))


class Copies:
    def __init__(self, send_sems, recv_sems, local_sems):
        self.send_sems, self.recv_sems, self.local_sems = send_sems, recv_sems, local_sems
        self.count = self.local_count = 0
        self.started = []

    def send(self, source, target, peer):
        copy = pltpu.make_async_remote_copy(
            src_ref=source,
            dst_ref=target,
            send_sem=self.send_sems.at[self.count],
            recv_sem=self.recv_sems.at[self.count],
            device_id=peer,
            device_id_type=MESH,
        )
        self.count += 1
        copy.start()
        self.started.append(copy)
        return copy

    def local(self, source, target):
        copy = pltpu.make_async_copy(source, target, self.local_sems.at[self.local_count])
        self.local_count += 1
        copy.start()
        return copy

    def finish(self):
        for copy in self.started:
            copy.wait_send()


class Ring:
    def __init__(self, at, net, own, slots):
        self.at, self.net, self.slots = at, net, slots
        self.up = net.send(own, slots.at[1], at.to_x(1))
        self.down = net.send(own, slots.at[2], at.to_x(3))
        self.far = []

    def forward(self):
        at, net, slots = self.at, self.net, self.slots
        half = slots.shape[1] // 2
        for copy, s, start, peer in (
            (self.up, 1, 0, at.to_x(1)),
            (self.down, 2, half, at.to_x(3)),
        ):
            copy.wait_recv()
            rows = pl.ds(start, half)
            self.far.append(net.send(slots.at[s, rows], slots.at[3, rows], peer))

    def wait(self):
        for copy in self.far:
            copy.wait_recv()


def greet(peers):
    barrier = pltpu.get_barrier_semaphore()
    for peer in peers:
        pl.semaphore_signal(barrier, inc=1, device_id=peer, device_id_type=MESH)
    pl.semaphore_wait(barrier, len(peers))


def lanes(shape):
    return lax.broadcasted_iota(jnp.int32, shape, len(shape) - 1)


def wheel(table):
    lane = lanes(table.shape)
    other = pltpu.roll(table, 64, 1)
    twice = jnp.concatenate(
        [jnp.where(lane < 64, table, other), jnp.where(lane < 64, other, table)], axis=0
    )
    turned = pltpu.roll(twice, 32, 1)
    first = lax.rem(lanes(twice.shape), 64) < 32
    return jnp.where(first, twice, turned), jnp.where(first, -turned, twice)


def turn(field, cosine, sine):
    first = lax.rem(lanes(field.shape), 64) < 32
    other = jnp.where(first, pltpu.roll(field, 96, 1), pltpu.roll(field, 32, 1))
    return field * cosine + other * sine


def key_masks(meta, f, ctx):
    own = meta[f, pl.ds(ctx, 1), :]
    diagonal = lax.broadcasted_iota(jnp.int32, (128, 128), 0) == lanes((128, 128))
    query = jnp.sum(jnp.where(diagonal, own, 0.0), axis=1, keepdims=True)
    return [
        jnp.where(meta[f, pl.ds(j, 1), :] <= query, 0.0, -1e30).astype(F32) for j in range(8)
    ]


def forward_kernel(
    meta_in,
    table_in,
    tok_in,
    q_in,
    k_in,
    v_in,
    o_in,
    gate_in,
    up_in,
    down_in,
    dy_in,
    meta,
    table,
    normed_out,
    queries_out,
    keys_out,
    logs_out,
    mixed_out,
    residual,
    normed_two,
    first_out,
    out_out,
    w_feed,
    w_down,
    dy,
    tok,
    normed,
    queries,
    keys,
    logs,
    mixed,
    own_two,
    w_first,
    w_out,
    sums,
    got,
    got_far,
    mask,
    stage_feed,
    stage_down,
    stage_dy,
    send_sems,
    recv_sems,
    local_sems,
):
    at = Spot()
    net = Copies(send_sems, recv_sems, local_sems)
    near = (1, 3, 2)
    slot = {1: 1, 3: 2, 2: 3}
    owner = {0: 0, 1: 3, 2: 1, 3: 2}
    greet(
        [at.fsdp(d) for d in range(1, 16)]
        + [at.to_y(d) for d in near]
        + [at.z_out(), at.z_hi()]
    )

    quarter = pl.ds(pl.multiple_of(at.y * 32, 32), 32)

    def first_parts(d, rows):
        rank = at.xs(d)
        half = pl.ds(pl.multiple_of(rank // 2 * 128, 128), 128)
        return (
            (q_in.at[rows, pl.ds(pl.multiple_of(rank * 512, 128), 512)], pl.ds(0, 512)),
            (k_in.at[rows, half], pl.ds(512, 128)),
            (v_in.at[rows, half], pl.ds(640, 128)),
        )

    def feed_parts(d, rows):
        span = pl.ds(pl.multiple_of(at.xs(d) * 1408, 128), 1408)
        return (
            (gate_in.at[rows, span], pl.ds(0, 1408)),
            (up_in.at[rows, span], pl.ds(1408, 1408)),
        )

    everything = pl.ds(0, 128)

    def spread(parts, full, stage):
        mine = [net.local(s, stage.at[:, t]) for s, t in parts(0, everything)]
        away = {
            d: [
                net.send(s, full.at[at.x, at.z, at.c, quarter, t], at.to_x(d))
                for s, t in parts(d, quarter)
            ]
            for d in near
        }
        return mine, away

    def share(full, away, d):
        for copy in away[d]:
            copy.wait_recv()
        block = full.at[at.xs(4 - d), at.z, at.c, quarter]
        return [net.send(block, block, at.to_y(e)) for e in near]

    def relay(full, d, source=None):
        block = full.at[at.xs(4 - d), at.z, at.c]
        source = block if source is None else source
        z = net.send(source, block, at.z_in() if d in (0, 2) else at.z_out())
        return z, net.send(source, block, at.core())

    def relay_core(full, d):
        block = full.at[at.xs(4 - d), 1 - at.z, at.c]
        return net.send(block, block, at.core())

    own_first = w_first.at[at.x, at.z, at.c]
    first_mine, first_away = spread(first_parts, w_first, own_first)
    tok_ring = Ring(at, net, tok_in, tok)
    own_tok = net.local(tok_in, tok.at[0])
    meta_copies = [net.send(meta_in, meta.at[at.f], at.fsdp(d)) for d in range(1, 16)]
    own_meta = net.local(meta_in, meta.at[at.f])
    table_copies = [net.send(table_in, table.at[slot[d]], at.to_x(d)) for d in near]
    own_table = net.local(table_in, table.at[0])
    for copy in first_mine:
        copy.wait()
    first_hops = {0: relay(w_first, 0)}
    first_shared = {d: share(w_first, first_away, d) for d in near}
    feed_mine, feed_away = spread(feed_parts, w_feed, stage_feed)
    own_out = net.local(o_in, w_out.at[at.z, at.c])
    load_down = net.local(down_in, stage_down)
    load_dy = net.local(dy_in, stage_dy)
    out_z = [
        net.send(o_in.at[pl.ds(0, 64)], w_out.at[at.z, at.c, pl.ds(0, 64)], at.z_in()),
        net.send(o_in.at[pl.ds(64, 64)], w_out.at[at.z, at.c, pl.ds(64, 64)], at.z_out()),
    ]
    out_c = [net.send(o_in, w_out.at[at.z, at.c], at.core())]
    for d in near:
        for copy in first_shared[d]:
            copy.wait_recv()
        first_hops[d] = relay(w_first, d)
    for copy in feed_mine:
        copy.wait()
    store = [net.local(stage_feed, w_feed.at[at.x, at.z, at.c])]
    feed_hops = {0: relay(w_feed, 0, stage_feed)}
    tok_ring.forward()
    dy_ring = Ring(at, net, dy_in, dy)
    load_down.wait()
    load_dy.wait()
    store.append(net.local(stage_down, w_down.at[at.z, at.c]))
    store.append(net.local(stage_dy, dy.at[0]))
    first_last = []
    for d in (0, *near):
        first_hops[d][0].wait_recv()
        first_last.append(relay_core(w_first, d))
    feed_shared = {d: share(w_feed, feed_away, d) for d in near}

    own_meta.wait()
    own_tok.wait()
    own_table.wait()
    tok_ring.wait()
    for copy in (*meta_copies, *table_copies):
        copy.wait_recv()
    for hop in first_hops.values():
        hop[1].wait_recv()
    for copy in first_last:
        copy.wait_recv()
    odd = lax.rem(at.x, 2) == 1

    def project(s, carry):
        values = tok[s].astype(F32)
        scale = lax.rsqrt(jnp.mean(values * values, axis=-1, keepdims=True) + epsilon)
        total = jnp.zeros((128, 768), F32)
        for f in range(16):
            span = pl.ds(f * 128, 128)
            normed[s, :, span] = (tok[s, :, span].astype(F32) * scale * meta[f, 8:9, :]).astype(BF)
        for g in range(8):
            total += dot(
                normed[s, :, pl.ds(g * 256, 256)],
                w_first[g // 2, g % 2].reshape(256, 768),
            )
        cosine, sine = wheel(table[s])
        for t in range(4):
            span = slice(t * 128, t * 128 + 128)
            queries[s, :, span] = (turn(total[:, span], cosine, sine) * 0.125).astype(BF)
        key, value = total[:, 512:640], total[:, 640:768]
        key = turn(jnp.where(odd, pltpu.roll(key, 64, 1), key), cosine, sine)
        value = jnp.where(odd, value, pltpu.roll(value, 64, 1))
        keys[s, at.ctx] = jnp.where(lanes((128, 128)) < 64, key, value).astype(BF)
        return carry

    lax.fori_loop(0, 4, project, 0)
    store += [net.local(w_first, first_out), net.local(normed, normed_out)]
    store.append(net.local(queries, queries_out))
    mine = keys.at[:, at.ctx]
    over = net.send(mine, mine, at.z_hi())
    key_copies = [net.send(mine, mine, at.to_y(d)) for d in near]
    down_z = [
        net.send(down_in.at[pl.ds(0, 176)], w_down.at[at.z, at.c, pl.ds(0, 176)], at.z_in()),
        net.send(down_in.at[pl.ds(176, 176)], w_down.at[at.z, at.c, pl.ds(176, 176)], at.z_out()),
    ]
    down_c = [net.send(down_in, w_down.at[at.z, at.c], at.core())]
    dy_ring.forward()
    over.wait_recv()
    theirs = keys.at[:, (1 - at.hi) * 4 + at.y]
    key_copies += [net.send(theirs, theirs, at.to_y(d)) for d in near]
    for d in near:
        for copy in feed_shared[d]:
            copy.wait_recv()
        feed_hops[d] = relay(w_feed, d)
    own_out.wait()
    for copy in out_z:
        copy.wait_recv()
    out_c.append(net.send(w_out.at[1 - at.z, at.c], w_out.at[1 - at.z, at.c], at.core()))
    for copy in out_c:
        copy.wait_recv()
    for copy in key_copies:
        copy.wait_recv()
    store += [net.local(keys, keys_out), net.local(w_out, out_out)]

    def attend(s):
        masks = key_masks(meta, at.xs(owner[s]) * 4 + at.zc, at.ctx)
        for j in range(8):
            mask[:, j * 128 : j * 128 + 128] = masks[j]
        both = keys[s].reshape(1024, 128).astype(F32)
        lane = lanes(both.shape)
        key = jnp.where(lane < 64, both, 0.0)
        value = jnp.where(lane < 64, 0.0, both)
        key_pair = (key.astype(BF), pltpu.roll(key, 64, 1).astype(BF))
        value_pair = (pltpu.roll(value, 64, 1).astype(BF), value.astype(BF))
        head_lane = lanes((128, 128))
        log_rows = jnp.zeros((128, 128), F32)
        for t in range(4):
            query = queries[s, :, t * 128 : t * 128 + 128]
            total = jnp.zeros((128, 128), F32)
            for p in range(2):
                scores = dot_t(query, key_pair[p]) + mask[...]
                largest = jnp.max(scores, axis=-1, keepdims=True)
                weights = jnp.exp(scores - largest)
                amount = jnp.sum(weights, axis=-1, keepdims=True)
                total += dot(weights.astype(BF), value_pair[p]) * (1.0 / amount)
                log_rows = jnp.where(
                    head_lane == 2 * t + p, largest + jnp.log(amount), log_rows
                )
            mixed[s, :, t * 128 : t * 128 + 128] = total.astype(BF)
        logs[s] = log_rows
        return dot(mixed[s], w_out[...].reshape(512, 2048))

    low, high = pl.ds(0, 64), pl.ds(64, 64)
    sums[2] = attend(3).astype(BF)
    passed = [
        net.send(sums.at[2, low], got_far.at[0], at.to_x(1)),
        net.send(sums.at[2, high], got_far.at[1], at.to_x(3)),
    ]
    sums[0] = attend(1).astype(BF)
    sum_copies = [net.send(sums.at[0, low], got.at[0, low], at.to_x(3))]
    sums[1] = attend(2).astype(BF)
    sum_copies.append(net.send(sums.at[1, high], got.at[1, high], at.to_x(1)))
    for i, (to, rows, peer) in enumerate(((1, low, at.to_x(1)), (0, high, at.to_x(3)))):
        passed[i].wait_recv()
        sums[to, rows] = (sums[to, rows].astype(F32) + got_far[i].astype(F32)).astype(BF)
        sum_copies.append(net.send(sums.at[to, rows], got.at[to, rows], peer))
    own = attend(0)
    store += [net.local(mixed, mixed_out), net.local(logs, logs_out)]
    feed_last = []
    for d in (0, *near):
        feed_hops[d][0].wait_recv()
        feed_last.append(relay_core(w_feed, d))
    for copy in sum_copies:
        copy.wait_recv()
    total = tok[0].astype(F32) + own
    for i in range(2):
        total += got[i].astype(F32)
    residual[...] = total
    scale = lax.rsqrt(jnp.mean(total * total, axis=-1, keepdims=True) + epsilon)
    for f in range(16):
        span = pl.ds(f * 128, 128)
        own_two[:, span] = (residual[:, span] * scale * meta[f, 9:10, :]).astype(BF)
    two_ring = Ring(at, net, own_two, normed_two)
    store.append(net.local(own_two, normed_two.at[0]))
    for copy in down_z:
        copy.wait_recv()
    down_c.append(net.send(w_down.at[1 - at.z, at.c], w_down.at[1 - at.z, at.c], at.core()))
    two_ring.forward()
    for copy in store:
        copy.wait()
    for hop in feed_hops.values():
        hop[1].wait_recv()
    for copy in (*down_c, *feed_last):
        copy.wait_recv()
    dy_ring.wait()
    two_ring.wait()
    net.finish()


def forward(meta, table, tok, q, k, v, o, gate, up, down, dy):
    shape = jax.ShapeDtypeStruct
    outs = (
        shape((16, 16, 128), F32),
        shape((4, 64, 128), F32),
        shape((4, 128, 2048), BF),
        shape((4, 128, 512), BF),
        shape((4, 8, 128, 128), BF),
        shape((4, 128, 128), F32),
        shape((4, 128, 512), BF),
        shape((128, 2048), F32),
        shape((4, 128, 2048), BF),
        shape((4, 2, 2, 128, 768), BF),
        shape((2, 2, 128, 2048), BF),
        shape((4, 2, 2, 128, 2816), BF),
        shape((2, 2, 352, 2048), BF),
        shape((4, 128, 2048), BF),
    )
    return pl.pallas_call(
        forward_kernel,
        name="forward",
        out_shape=outs,
        in_specs=[EVERYWHERE] * 11,
        out_specs=(ON_CHIP,) * 2 + (EVERYWHERE,) * 5 + (ON_CHIP,) + (EVERYWHERE,) * 6,
        scratch_shapes=[
            pltpu.VMEM((4, 128, 2048), BF),
            pltpu.VMEM((4, 128, 2048), BF),
            pltpu.VMEM((4, 128, 512), BF),
            pltpu.VMEM((4, 8, 128, 128), BF),
            pltpu.VMEM((4, 128, 128), F32),
            pltpu.VMEM((4, 128, 512), BF),
            pltpu.VMEM((128, 2048), BF),
            pltpu.VMEM((4, 2, 2, 128, 768), BF),
            pltpu.VMEM((2, 2, 128, 2048), BF),
            pltpu.VMEM((3, 128, 2048), BF),
            pltpu.VMEM((2, 128, 2048), BF),
            pltpu.VMEM((2, 64, 2048), BF),
            pltpu.VMEM((128, 1024), F32),
            pltpu.VMEM((128, 2816), BF),
            pltpu.VMEM((352, 2048), BF),
            pltpu.VMEM((128, 2048), BF),
            pltpu.SemaphoreType.DMA((112,)),
            pltpu.SemaphoreType.DMA((112,)),
            pltpu.SemaphoreType.DMA((32,)),
        ],
        compiler_params=pltpu.CompilerParams(
            collective_id=1, has_side_effects=True, vmem_limit_bytes=VMEM_LIMIT
        ),
    )(meta, table, tok, q, k, v, o, gate, up, down, dy)


NEAR = (1, 3, 2)
CHUNKS = ((0, 512), (512, 512), (1024, 384))


def feed_kernel(
    n2,
    dy,
    residual,
    meta,
    feed_in,
    down_in,
    part_out,
    dr,
    dz,
    keep_feed,
    keep_down,
    gain_term,
    w_feed,
    w_down,
    hid,
    dgu,
    part_two,
    got_two,
    part_y,
    core_feed,
    core_down,
    gain,
    send_sems,
    recv_sems,
    local_sems,
):
    at = Spot()
    net = Copies(send_sems, recv_sems, local_sems)
    loads = []
    for start, size in CHUNKS:
        spans = pl.ds(start, size), pl.ds(1408 + start, size)
        loads.append(
            [net.local(feed_in.at[..., t], w_feed.at[..., t]) for t in spans]
            + [net.local(down_in.at[spans[0]], w_down.at[spans[0]])]
        )
    greet([at.to_x(d) for d in NEAR] + [at.z_in(), at.z_out(), at.core()])
    for f in range(16):
        gain[:, f * 128 : f * 128 + 128] = meta[f, 9:10, :]

    two_copies = []
    for first in (2, 0):
        rows = slice(first * 128, first * 128 + 256)
        tokens_here = n2[first : first + 2].reshape(256, 2048)
        cotangent_here = dy[first : first + 2].reshape(256, 2048)
        for (start, size), load in zip(CHUNKS, loads):
            if first:
                for copy in load:
                    copy.wait()
            gate = jnp.zeros((256, size), F32)
            up = jnp.zeros((256, size), F32)
            for x in range(4):
                some = tokens_here[:, x * 512 : x * 512 + 512]
                gate += dot(some, w_feed[x, :, :, :, start : start + size].reshape(512, size))
                up += dot(
                    some,
                    w_feed[x, :, :, :, 1408 + start : 1408 + start + size].reshape(512, size),
                )
            dhid = dot_t(cotangent_here, w_down[start : start + size, :])
            sigmoid = 1.0 / (1.0 + jnp.exp(-gate))
            activated = gate * sigmoid
            hid[rows, start : start + size] = (activated * up).astype(BF)
            slope = sigmoid * (1.0 + gate * (1.0 - sigmoid))
            dgu[rows, start : start + size] = (dhid * up * slope).astype(BF)
            dgu[rows, 1408 + start : 1408 + start + size] = (dhid * activated).astype(BF)
        for x in range(4):
            span = slice(x * 512, x * 512 + 512)
            term = dot_t(dgu[rows, :], w_feed[x].reshape(512, 2816))
            part_two[first + 1, :, span] = term[128:].astype(BF)
            if first == 0:
                dr[:, span] = term[:128]
                two_copies.append(
                    net.send(part_two.at[1, :, span], got_two.at[0, :, span], at.to_x(3))
                )
            else:
                part_two[first, :, span] = term[:128].astype(BF)
        if first:
            for s, d in ((3, 2), (2, 1)):
                two_copies.append(net.send(part_two.at[s], got_two.at[s - 1], at.to_x(d)))

    core_copies, z_copies, stores = [], [], []

    def pass_z(x):
        core_copies[x].wait_recv()
        w_feed[x, 1 - at.z, at.c] = (
            w_feed[x, 1 - at.z, at.c].astype(F32) + core_feed[x, 1 - at.z].astype(F32)
        ).astype(BF)
        z_copies.append(
            net.send(
                w_feed.at[x, 1 - at.z, at.c],
                keep_feed.at[x],
                at.z_out() if x % 2 else at.z_in(),
            )
        )

    for x in range(4):
        some = n2[:, :, x * 512 : x * 512 + 512].reshape(512, 512)
        for start, size in ((0, 1408), (1408, 1408)):
            w_feed[x, :, :, :, start : start + size] = (
                t_dot(some, dgu[:, start : start + size])
                .astype(BF)
                .reshape(2, 2, 128, size)
            )
        core_copies.append(net.send(w_feed.at[x, :, 1 - at.c], core_feed.at[x], at.core()))
        if x:
            pass_z(x - 1)
    for first in (2, 0):
        rows = slice(first * 128, first * 128 + 256)
        for j in range(4):
            span = slice(j * 512, j * 512 + 512)
            term = dot(hid[rows, :], w_down[:, span]).astype(BF)
            part_y[first, :, span] = term[:128]
            part_y[first + 1, :, span] = term[128:]
        pair = pl.ds(first, 2)
        stores.append(net.local(part_y.at[pair], part_out.at[pair]))
        if first:
            pass_z(3)

    for copy in two_copies:
        copy.wait_recv()
    grad = dr[...]
    for i in range(3):
        grad += got_two[i].astype(F32)
    values = residual[...]
    scale = lax.rsqrt(jnp.mean(values * values, axis=-1, keepdims=True) + epsilon)
    gain_term[...] = jnp.sum(grad * values * scale, axis=0, keepdims=True)
    weighted = grad * gain[...]
    inner = jnp.mean(weighted * values, axis=-1, keepdims=True)
    dr[...] = dy[0].astype(F32) + weighted * scale - values * (scale * scale * scale * inner)
    dz[0] = dr[...].astype(BF)
    ring = Ring(at, net, dz.at[0], dz)

    for start, size in CHUNKS:
        w_down[start : start + size, :] = t_dot(
            hid[:, start : start + size], dy[...].reshape(512, 2048)
        ).astype(BF)

    def down_rows(z, c):
        return pl.ds(pl.multiple_of((z * 2 + c) * 352, 16), 352)

    down_copies = [
        net.send(w_down.at[down_rows(z, 1 - at.c)], core_down.at[z], at.core()) for z in range(2)
    ]
    ring.forward()
    for z in range(2):
        down_copies[z].wait_recv()
    for i, z in enumerate((at.z, 1 - at.z)):
        keep_down[i] = (
            w_down[down_rows(z, at.c), :].astype(F32) + core_down[z].astype(F32)
        ).astype(BF)
    for x in range(4):
        z_copies[x].wait_recv()
        keep_feed[x] = (
            keep_feed[x].astype(F32)
            + w_feed[x, at.z, at.c].astype(F32)
            + core_feed[x, at.z].astype(F32)
        ).astype(BF)
    ring.wait()
    for copy in stores:
        copy.wait()
    net.finish()


def feed(n2, dy, residual, meta, w_feed, w_down):
    shape = jax.ShapeDtypeStruct
    return pl.pallas_call(
        feed_kernel,
        name="feed",
        out_shape=(
            shape((4, 128, 2048), BF),
            shape((128, 2048), F32),
            shape((4, 128, 2048), BF),
            shape((4, 128, 2816), BF),
            shape((2, 352, 2048), BF),
            shape((1, 2048), F32),
        ),
        in_specs=[ON_CHIP] * 4 + [EVERYWHERE] * 2,
        out_specs=(EVERYWHERE,) + (ON_CHIP,) * 5,
        scratch_shapes=[
            pltpu.VMEM((4, 2, 2, 128, 2816), BF),
            pltpu.VMEM((1408, 2048), BF),
            pltpu.VMEM((512, 1408), BF),
            pltpu.VMEM((512, 2816), BF),
            pltpu.VMEM((4, 128, 2048), BF),
            pltpu.VMEM((3, 128, 2048), BF),
            pltpu.VMEM((4, 128, 2048), BF),
            pltpu.VMEM((4, 2, 128, 2816), BF),
            pltpu.VMEM((2, 352, 2048), BF),
            pltpu.VMEM((1, 2048), F32),
            pltpu.SemaphoreType.DMA((32,)),
            pltpu.SemaphoreType.DMA((32,)),
            pltpu.SemaphoreType.DMA((16,)),
        ],
        compiler_params=pltpu.CompilerParams(
            collective_id=2, has_side_effects=True, vmem_limit_bytes=VMEM_LIMIT
        ),
    )(n2, dy, residual, meta, w_feed, w_down)


class Sums:
    def __init__(self, at, net):
        self.at, self.net = at, net

    def over_y(self, halves, own, relay, joined, got, out):
        at, net = self.at, self.net
        up, down, far = halves(at.ys(1)), halves(at.ys(3)), halves(at.ys(2))
        passed = [
            net.send(far[0], relay[0], at.to_y(1)),
            net.send(far[1], relay[1], at.to_y(3)),
        ]
        copies = [
            net.send(up[1], got[0][1], at.to_y(1)),
            net.send(down[0], got[1][0], at.to_y(3)),
        ]
        yield
        for i, (source, target, peer) in enumerate(
            ((up[0], got[0][0], at.to_y(1)), (down[1], got[1][1], at.to_y(3)))
        ):
            passed[i].wait_recv()
            joined[i][...] = (source[...].astype(F32) + relay[i][...].astype(F32)).astype(BF)
            copies.append(net.send(joined[i], target, peer))
        yield
        for copy in copies:
            copy.wait_recv()
        for h in range(2):
            out[h][...] = (
                own[h][...].astype(F32) + got[0][h][...].astype(F32) + got[1][h][...].astype(F32)
            ).astype(BF)

    def around_y(self, halves):
        at, net = self.at, self.net
        copies = [net.send(h, h, at.to_y(d)) for d in (1, 3) for h in halves(at.y)]
        yield
        copies[0].wait_recv()
        far = halves(at.ys(3))[0]
        last = [net.send(far, far, at.to_y(1))]
        copies[3].wait_recv()
        far = halves(at.ys(1))[1]
        last.append(net.send(far, far, at.to_y(3)))
        yield
        for copy in (copies[1], copies[2], *last):
            copy.wait_recv()

    def over_z_hi(self, mine, got):
        copy = self.net.send(mine, got, self.at.z_hi())
        yield
        copy.wait_recv()
        got[...] = (got[...].astype(F32) + mine[...].astype(F32)).astype(BF)

    def columns(self, terms, span, relay, joined, got_y, mine, got_z, place, halves):
        at, net = self.at, self.net

        def parts(y):
            rows = pl.ds(pl.multiple_of(y * 32, 32), 32)
            return [terms.at[h : h + 2, rows, span] for h in (0, 2)]

        pair = lambda ref: [ref.at[h : h + 2, :, span] for h in (0, 2)]
        ends = lambda ref: [ref.at[i, :, :, span] for i in range(2)]
        yield from self.over_y(
            parts,
            parts(at.y),
            ends(relay),
            ends(joined),
            [pair(got_y.at[i]) for i in range(2)],
            pair(mine),
        )
        yield from self.over_z_hi(mine.at[:, :, span], got_z.at[:, :, span])
        here = net.local(got_z.at[at.x, :, span], place(at.x))
        copies = [
            net.send(got_z.at[at.xs(d), :, span], place(at.x), at.to_x(d)) for d in NEAR
        ]
        here.wait()
        yield
        for copy in copies:
            copy.wait_recv()
        yield from self.around_y(halves)

    def rows(self, terms, relay, joined, got_y, mine, got_z, out):
        at, net = self.at, self.net
        half = terms.shape[0] // 2
        starts = (0, half)

        def split(ref, y):
            columns = pl.ds(pl.multiple_of(y * 512, 128), 512)
            return [ref.at[pl.ds(h, half), columns] for h in starts]

        pair = lambda ref: [ref.at[pl.ds(h, half)] for h in starts]
        yield from self.over_y(
            lambda y: split(terms, y),
            split(terms, at.y),
            [relay.at[i] for i in range(2)],
            [joined.at[i] for i in range(2)],
            [pair(got_y.at[i]) for i in range(2)],
            pair(mine),
        )
        yield from self.over_z_hi(mine, got_z)
        here = [
            net.local(got_z.at[pl.ds(h, half)], place)
            for h, place in zip(starts, split(out, at.y))
        ]
        for copy in here:
            copy.wait()
        yield from self.around_y(lambda y: split(out, y))

    def down(self, terms, got_z):
        at, net = self.at, self.net
        copies = [
            net.send(terms.at[1, pl.ds(r, 176)], got_z.at[pl.ds(r, 176)], peer)
            for r, peer in ((0, at.z_in()), (176, at.z_out()))
        ]
        yield
        for copy in copies:
            copy.wait_recv()
        got_z[...] = (got_z[...].astype(F32) + terms[0].astype(F32)).astype(BF)

    def first(self, terms, span, got_core, got_z):
        at, net = self.at, self.net
        copy = net.send(
            terms.at[:, :, 1 - at.c, :, span], got_core.at[:, :, :, span], at.core()
        )
        yield
        copy.wait_recv()
        for r in range(4):
            terms[r, 1 - at.z, at.c, :, span] = (
                terms[r, 1 - at.z, at.c, :, span].astype(F32)
                + got_core[r, 1 - at.z, :, span].astype(F32)
            ).astype(BF)
        copies = [
            net.send(
                terms.at[r : r + 2, 1 - at.z, at.c, :, span], got_z.at[r : r + 2, :, span], peer
            )
            for r, peer in ((0, at.z_in()), (2, at.z_out()))
        ]
        yield
        for copy in copies:
            copy.wait_recv()
        for r in range(4):
            got_z[r, :, span] = (
                got_z[r, :, span].astype(F32)
                + terms[r, at.z, at.c, :, span].astype(F32)
                + got_core[r, at.z, :, span].astype(F32)
            ).astype(BF)

    def out(self, terms, got_core, got_z):
        at, net = self.at, self.net
        copy = net.send(terms.at[:, 1 - at.c], got_core, at.core())
        yield
        copy.wait_recv()
        terms[1 - at.z, at.c] = (
            terms[1 - at.z, at.c].astype(F32) + got_core[1 - at.z].astype(F32)
        ).astype(BF)
        copies = [
            net.send(
                terms.at[1 - at.z, at.c, pl.ds(r, 64)], got_z.at[pl.ds(r, 64)], peer
            )
            for r, peer in ((0, at.z_in()), (64, at.z_out()))
        ]
        yield
        for copy in copies:
            copy.wait_recv()
        got_z[...] = (
            got_z[...].astype(F32)
            + terms[at.z, at.c].astype(F32)
            + got_core[at.z].astype(F32)
        ).astype(BF)


def chained(*parts):
    for part in parts:
        yield from part


def backward_kernel(
    dz,
    dr_in,
    tok,
    meta,
    table,
    queries,
    keys,
    logs,
    mixed,
    normed_in,
    first_in,
    w_out,
    feed_terms,
    down_terms,
    gain_two,
    part_y,
    residual_in,
    dx,
    output,
    gains,
    gate_sum,
    up_sum,
    down_sum,
    out_sum,
    first_sum,
    dr,
    own_y,
    residual,
    normed,
    w_first,
    got_out,
    dmix,
    mask,
    probs,
    scores_grad,
    pre,
    key_part,
    key_got,
    part,
    got_part,
    out_terms,
    out_core,
    out_z,
    first_terms,
    first_core,
    first_z,
    feed_r,
    feed_j,
    feed_y,
    feed_mine,
    feed_z,
    down_zz,
    down_r,
    down_j,
    down_y,
    down_mine,
    down_z,
    out_r,
    out_j,
    out_y,
    out_mine,
    out_zz,
    first_r,
    first_j,
    first_y,
    first_mine,
    first_zz,
    gain,
    gain_send,
    gain_got,
    gain_part,
    gain_last,
    send_sems,
    recv_sems,
    local_sems,
):
    at = Spot()
    net = Copies(send_sems, recv_sems, local_sems)
    slot = {1: 1, 3: 2, 2: 3}
    owner = {0: 0, 1: 3, 2: 1, 3: 2}

    def to_ctx(k):
        return (lax.rem(at.ctx + k, 8), at.f)

    load_normed = net.local(normed_in, normed)
    load_first = net.local(first_in, w_first)
    load_rest = [
        net.local(dr_in, dr),
        net.local(part_y.at[0], own_y),
        net.local(residual_in, residual),
    ]
    greet(
        [at.fsdp(d) for d in range(1, 16)] + [to_ctx(k) for k in range(1, 8)] + [at.z_out()]
    )
    sums = Sums(at, net)

    def rows_of(y):
        return pl.ds(pl.multiple_of(y * 32, 32), 32)

    def feed_chain(span, out):
        return sums.columns(
            feed_terms,
            span,
            feed_r,
            feed_j,
            feed_y,
            feed_mine,
            feed_z,
            lambda r: out.at[rows_of(at.y), pl.ds(pl.multiple_of(r * 1408, 128), 1408)],
            lambda y: [out.at[rows_of(y), pl.ds(h, 2816)] for h in (0, 2816)],
        )

    gate_chain = feed_chain(slice(0, 1408), gate_sum)
    up_chain = feed_chain(slice(1408, 2816), up_sum)
    down_chain = chained(
        sums.down(down_terms, down_zz),
        sums.rows(down_zz, down_r, down_j, down_y, down_mine, down_z, down_sum),
    )
    out_chain = chained(
        sums.out(out_terms, out_core, out_z),
        sums.rows(out_z, out_r, out_j, out_y, out_mine, out_zz, out_sum),
    )

    def first_chain(span):
        return chained(
            sums.first(first_terms, span, first_core, first_z),
            sums.columns(
                first_z,
                span,
                first_r,
                first_j,
                first_y,
                first_mine,
                first_zz,
                lambda r: first_sum.at[r, rows_of(at.y), span],
                lambda y: [first_sum.at[h : h + 2, rows_of(y), span] for h in (0, 2)],
            ),
        )

    query_chain = first_chain(slice(0, 512))
    key_chain = first_chain(slice(512, 640))

    def step(*chains):
        for chain in chains:
            next(chain, None)

    step(gate_chain, down_chain)
    y_copies = [
        net.send(part_y.at[s], got_out.at[s - 1], at.to_x(d)) for s, d in ((3, 2), (1, 3), (2, 1))
    ]
    for f in range(16):
        gain[:, f * 128 : f * 128 + 128] = meta[f, 8:9, :]
    weight = w_out[...].reshape(512, 2048)
    for s in range(4):
        dmix[s] = dot_t(dz[s], weight).astype(BF)
    for j in range(2):
        span = slice(j * 1024, j * 1024 + 1024)
        out_terms[:, :, :, span] = (
            t_dot(mixed[...].reshape(512, 512), dz[:, :, span].reshape(512, 1024))
            .astype(BF)
            .reshape(2, 2, 128, 1024)
        )
    step(out_chain)

    def attend(s):
        masks = key_masks(meta, at.xs(owner[s]) * 4 + at.zc, at.ctx)
        for j in range(8):
            mask[:, j * 128 : j * 128 + 128] = masks[j]
        both = keys[s].reshape(1024, 128).astype(F32)
        lane = lanes(both.shape)
        key = jnp.where(lane < 64, both, 0.0)
        value = jnp.where(lane < 64, 0.0, both)
        key_pair = (key.astype(BF), pltpu.roll(key, 64, 1).astype(BF))
        value_pair = (pltpu.roll(value, 64, 1).astype(BF), value.astype(BF))
        cosine, sine = wheel(table[s])
        for t in range(4):
            span = slice(t * 128, t * 128 + 128)
            query, grad = queries[s, :, span], dmix[s, :, span]
            total = jnp.zeros((128, 128), F32)
            for p in range(2):
                scores = dot_t(query, key_pair[p]) + mask[...]
                prob = jnp.exp(scores - logs[s, :, 2 * t + p : 2 * t + p + 1])
                prob_grad = dot_t(grad, value_pair[p])
                inner = jnp.sum(prob * prob_grad, axis=-1, keepdims=True)
                low = (prob * (prob_grad - inner)).astype(BF)
                probs[p, span, :] = prob.astype(BF)
                scores_grad[p, span, :] = low
                total += dot(low, key_pair[p])
            pre[s, :, span] = turn(total * 0.125, cosine, -sine).astype(BF)
        stack = lambda a: jnp.concatenate([a[s, :, t * 128 : t * 128 + 128] for t in range(4)], axis=0)
        query, grad = stack(queries), stack(dmix)
        half = lanes((1024, 128)) < 64
        key_grad = t_dot(scores_grad[0], query), t_dot(scores_grad[1], query)
        value_grad = t_dot(probs[0], grad), t_dot(probs[1], grad)
        total = jnp.where(
            half,
            key_grad[0] + pltpu.roll(key_grad[1], 64, 1),
            pltpu.roll(value_grad[0], 64, 1) + value_grad[1],
        )
        for j in range(8):
            key_part[j, s] = total[j * 128 : j * 128 + 128].astype(BF)

    def send_keys(first):
        return [
            net.send(
                key_part.at[lax.rem(at.ctx + k, 8), first : first + 2],
                key_got.at[k - 1, first : first + 2],
                to_ctx(k),
            )
            for k in range(1, 8)
        ]

    attend(0)
    step(out_chain, gate_chain, up_chain)
    attend(1)
    key_copies = send_keys(0)
    step(gate_chain)
    attend(2)
    step(out_chain, up_chain, gate_chain, down_chain)
    attend(3)
    key_copies += send_keys(2)
    step(gate_chain, up_chain)
    load_normed.wait()
    for x in range(4):
        first_terms[x, :, :, :, 0:512] = (
            t_dot(
                normed[:, :, x * 512 : x * 512 + 512].reshape(512, 512),
                pre[:, :, 0:512].reshape(512, 512),
            )
            .astype(BF)
            .reshape(2, 2, 128, 512)
        )
    step(query_chain, up_chain, query_chain, out_chain, down_chain, gate_chain)
    for copy in key_copies:
        copy.wait_recv()
    odd = lax.rem(at.x, 2) == 1
    half = lanes((128, 128)) < 64
    windows = []
    for s in range(4):
        total = key_part[at.ctx, s].astype(F32)
        for k in range(7):
            total += key_got[k, s].astype(F32)
        cosine, sine = wheel(table[s])
        total = jnp.where(half, turn(total, cosine, -sine), total)
        pre[s, :, 512:640] = total.astype(BF)
        moved = pltpu.roll(total, 64, 1)
        windows.append(
            jnp.concatenate(
                [
                    jnp.where(half, jnp.where(odd, 0.0, total), jnp.where(odd, moved, 0.0)),
                    jnp.where(half, jnp.where(odd, 0.0, moved), jnp.where(odd, total, 0.0)),
                ],
                axis=1,
            ).astype(BF)
        )
    window = jnp.concatenate(windows, axis=0)
    load_first.wait()
    for x in range(4):
        span = slice(x * 512, x * 512 + 512)
        term = dot_t(
            pre[:, :, 0:512].reshape(512, 512), w_first[x, :, :, :, 0:512].reshape(512, 512)
        ) + dot_t(window, w_first[x, :, :, :, 512:768].reshape(512, 256))
        dx[:, span] = term[:128]
        for s in range(1, 4):
            part[s, :, span] = term[s * 128 : s * 128 + 128].astype(BF)
    part_copies = [
        net.send(part.at[s], got_part.at[s - 1], at.to_x(d)) for s, d in ((3, 2), (1, 3), (2, 1))
    ]
    for x in range(4):
        first_terms[x, :, :, :, 512:640] = (
            t_dot(
                normed[:, :, x * 512 : x * 512 + 512].reshape(512, 512),
                pre[:, :, 512:640].reshape(512, 128),
            )
            .astype(BF)
            .reshape(2, 2, 128, 128)
        )
    step(key_chain, query_chain, key_chain, up_chain, down_chain, out_chain)
    for copy in load_rest:
        copy.wait()
    for copy in y_copies:
        copy.wait_recv()
    total = residual[...] + own_y[...].astype(F32)
    for i in range(3):
        total += got_out[i].astype(F32)
    output[...] = total.astype(BF)
    step(key_chain, query_chain, down_chain, up_chain)
    for copy in part_copies:
        copy.wait_recv()
    grad = dx[...]
    for i in range(3):
        grad += got_part[i].astype(F32)
    values = tok[...].astype(F32)
    scale = lax.rsqrt(jnp.mean(values * values, axis=-1, keepdims=True) + epsilon)
    gain_one = jnp.sum(grad * values * scale, axis=0, keepdims=True)
    weighted = grad * gain[...]
    inner = jnp.mean(weighted * values, axis=-1, keepdims=True)
    dx[...] = dr[...] + weighted * scale - values * (scale * scale * scale * inner)
    for f in range(16):
        span = slice(f * 128, f * 128 + 128)
        gain_send[f] = jnp.concatenate(
            [gain_one[:, span], gain_two[:, span], jnp.zeros((6, 128), F32)], axis=0
        )
    gain_copies = [
        net.send(gain_send.at[lax.rem(at.f + d, 16)], gain_got.at[d - 1], at.fsdp(d))
        for d in range(1, 16)
    ]
    everyone = (key_chain, query_chain, gate_chain, up_chain, down_chain, out_chain)
    step(*everyone)
    for copy in gain_copies:
        copy.wait_recv()
    total = gain_send[at.f]
    for d in range(15):
        total += gain_got[d]
    gain_part[...] = total
    last_copies = [net.send(gain_part, gain_last.at[k - 1], to_ctx(k)) for k in range(1, 8)]
    for _ in range(4):
        step(*everyone)
    for copy in last_copies:
        copy.wait_recv()
    total = gain_part[...]
    for k in range(7):
        total += gain_last[k]
    gains[...] = total
    for _ in range(8):
        step(*everyone)
    net.finish()


def backward(*operands):
    shape = jax.ShapeDtypeStruct
    vmem = lambda *dims: pltpu.VMEM(dims, BF)
    wide = lambda *dims: pltpu.VMEM(dims, F32)
    return pl.pallas_call(
        backward_kernel,
        name="backward",
        out_shape=(
            shape((128, 2048), F32),
            shape((128, 2048), BF),
            shape((8, 128), F32),
            shape((128, 5632), BF),
            shape((128, 5632), BF),
            shape((352, 2048), BF),
            shape((128, 2048), BF),
            shape((4, 128, 640), BF),
        ),
        in_specs=[ON_CHIP]
        + [EVERYWHERE]
        + [ON_CHIP] * 7
        + [EVERYWHERE] * 2
        + [ON_CHIP] * 4
        + [EVERYWHERE] * 2,
        out_specs=(ON_CHIP,) * 8,
        scratch_shapes=[
            wide(128, 2048),
            vmem(128, 2048),
            wide(128, 2048),
            vmem(4, 128, 2048),
            vmem(4, 2, 2, 128, 768),
            vmem(3, 128, 2048),
            vmem(4, 128, 512),
            wide(128, 1024),
            vmem(2, 512, 1024),
            vmem(2, 512, 1024),
            vmem(4, 128, 640),
            vmem(8, 4, 128, 128),
            vmem(7, 4, 128, 128),
            vmem(4, 128, 2048),
            vmem(3, 128, 2048),
            vmem(2, 2, 128, 2048),
            vmem(2, 128, 2048),
            vmem(128, 2048),
            vmem(4, 2, 2, 128, 640),
            vmem(4, 2, 128, 640),
            vmem(4, 128, 640),
            vmem(2, 2, 32, 2816),
            vmem(2, 2, 32, 2816),
            vmem(2, 4, 32, 2816),
            vmem(4, 32, 2816),
            vmem(4, 32, 2816),
            vmem(352, 2048),
            vmem(2, 176, 512),
            vmem(2, 176, 512),
            vmem(2, 352, 512),
            vmem(352, 512),
            vmem(352, 512),
            vmem(2, 64, 512),
            vmem(2, 64, 512),
            vmem(2, 128, 512),
            vmem(128, 512),
            vmem(128, 512),
            vmem(2, 2, 32, 640),
            vmem(2, 2, 32, 640),
            vmem(2, 4, 32, 640),
            vmem(4, 32, 640),
            vmem(4, 32, 640),
            wide(1, 2048),
            wide(16, 8, 128),
            wide(15, 8, 128),
            wide(8, 128),
            wide(7, 8, 128),
            pltpu.SemaphoreType.DMA((160,)),
            pltpu.SemaphoreType.DMA((160,)),
            pltpu.SemaphoreType.DMA((16,)),
        ],
        compiler_params=pltpu.CompilerParams(
            collective_id=3, has_side_effects=True, vmem_limit_bytes=VMEM_LIMIT
        ),
    )(*operands)


def finish_kernel(first, out, gate, up, down, query_f, key_f, value_f, out_f, gate_f, up_f, down_f):
    out_f[...] = out[...].astype(F32)
    gate_f[...] = gate[...].astype(F32)
    up_f[...] = up[...].astype(F32)
    down_f[...] = down[...].astype(F32)
    for r in range(4):
        query_f[:, r * 512 : r * 512 + 512] = first[r, :, 0:512].astype(F32)
    for r in (0, 2):
        low, high = first[r, :, 512:640].astype(F32), first[r + 1, :, 512:640].astype(F32)
        half = lanes(low.shape) < 64
        span = slice(r * 64, r * 64 + 128)
        key_f[:, span] = jnp.where(half, low, pltpu.roll(high, 64, 1))
        value_f[:, span] = jnp.where(half, pltpu.roll(low, 64, 1), high)


def finish(first, out, gate, up, down):
    flat = lambda rows, width: pl.BlockSpec((rows // 2, width), lambda i: (i, 0))
    sizes = ((128, 2048), (128, 256), (128, 256), (128, 2048), (128, 5632), (128, 5632), (352, 2048))
    return pl.pallas_call(
        finish_kernel,
        name="finish",
        grid=(2,),
        out_shape=[jax.ShapeDtypeStruct(size, F32) for size in sizes],
        in_specs=[pl.BlockSpec((4, 64, 640), lambda i: (0, i, 0))]
        + [flat(*size) for size in sizes[3:]],
        out_specs=[flat(*size) for size in sizes],
        compiler_params=pltpu.CompilerParams(vmem_limit_bytes=VMEM_LIMIT),
    )(first, out, gate, up, down)


def per_device(
    tokens,
    positions,
    attention_gain,
    query_weight,
    key_weight,
    value_weight,
    out_weight,
    feed_gain,
    gate_weight,
    up_weight,
    down_weight,
    cotangent,
):
    width = tokens.shape[3]
    places = positions.reshape(2, 8, 64).transpose(1, 0, 2).reshape(8, 128).astype(F32)
    meta = jnp.concatenate(
        [places, attention_gain[None], feed_gain[None], jnp.zeros((6, 128), F32)], axis=0
    )
    own_places = lax.dynamic_index_in_dim(places, lax.axis_index("ctx"), 0, keepdims=False)[:, None]
    angles = own_places * frequencies(HEAD_DIM)[None]
    table = jnp.concatenate(
        [jnp.cos(angles[:64]), jnp.sin(angles[:64]), jnp.cos(angles[64:]), jnp.sin(angles[64:])],
        axis=1,
    )
    token_rows = tokens.reshape(128, width)
    branch_grad = cotangent.reshape(128, width)
    (
        meta,
        table,
        normed,
        query_rot,
        keys,
        logs,
        mixed_low,
        residual,
        normed_two,
        w_first,
        w_out,
        w_feed,
        w_down,
        branch4,
    ) = forward(
        meta,
        table,
        token_rows,
        query_weight,
        key_weight,
        value_weight,
        out_weight,
        gate_weight,
        up_weight,
        down_weight,
        branch_grad,
    )
    part_y, residual_grad, branch_low, feed_terms, down_terms, gain_two_term = feed(
        normed_two, branch4, residual, meta, w_feed, w_down.reshape(1408, width)
    )
    input_grad, output, gains, gate_sum, up_sum, down_sum, out_sum, first_sum = backward(
        branch_low,
        residual_grad,
        token_rows,
        meta,
        table,
        query_rot,
        keys,
        logs,
        mixed_low,
        normed,
        w_first,
        w_out,
        feed_terms,
        down_terms,
        gain_two_term,
        part_y,
        residual,
    )
    sums = finish(first_sum, out_sum, gate_sum, up_sum, down_sum)
    return (
        output.reshape(tokens.shape),
        input_grad.reshape(tokens.shape),
        gains[0],
        *sums[:4],
        gains[1],
        *sums[4:],
    )


def solution(mesh):
    rows = P("fsdp", None)
    blocks = P("fsdp", None, "ctx", None)
    return jax.shard_map(
        per_device,
        mesh=mesh,
        in_specs=(
            blocks,
            P("fsdp", None, None),
            P("fsdp"),
            rows,
            rows,
            rows,
            rows,
            P("fsdp"),
            rows,
            rows,
            rows,
            blocks,
        ),
        out_specs=(blocks, blocks, P("fsdp"), rows, rows, rows, rows, P("fsdp"), rows, rows, rows),
        check_vma=False,
    )
```
